32 devices in a mesh: ent: 4 (over y, core), grp: 8 (over z, x).
Axes of the slice: x: 2, y: 2, z: 4, core: 2. Of those that a mesh axis runs over, the one named last changes fastest.
Arguments:
- table: float32 [65536, 512], P(('ent', 'grp')), may hold values from -6 to 6
- touch_owner: int32 [16384, 1], P(('ent', 'grp')), may hold values from 0 to 31; in each aligned block of 512 rows (0 to 511, 512 to 1023, ...) at most 32 rows name the same one
- touch_local: int32 [16384], P(('ent', 'grp')), may hold values from 0 to 2047
- query_rel: int32 [8192], P(('ent', 'grp')), may hold values from 0 to 821
- neg_local: int32 [8192], P(('ent', 'grp')), may hold values from 0 to 2047
- rel_table: bfloat16 [822, 512], replicated, may hold values from -6 to 6
- in_gain: float32 [512], replicated, may hold values from 0.1 to 1.9
- out_gain: float32 [512], replicated, may hold values from 0.1 to 1.9
- w_gate: bfloat16 [512, 2048], replicated, may hold values from -0.25 to 0.25
- w_up: bfloat16 [512, 2048], replicated, may hold values from -0.25 to 0.25
- w_down: bfloat16 [2048, 512], replicated, may hold values from -0.125 to 0.125
Outputs:
- table_grad: float32 [65536, 512], P(('ent', 'grp'))
The draws below stay inside these ranges and needn't reach their ends.
Inputs may be any that keep to these rules, and one draw needn't show every extreme that they name: `touch_owner`: in each device's block of 512 references no owner is named more than 32 times, a bound that some block reaches.
All inputs are finite; a program needn't handle non-finite values.
Results may differ from the reference program's by a relative error of at most 0.0085.
Values may be sent and summed in bfloat16 or wider, within the bound.
No kernel may reach another device: no remote copies, remote signals or barrier semaphores. Data moves between devices by JAX's collectives and lax.ppermute only.
A program may use at most 128 MiB of HBM per device.

```python
import math
import jax
import jax.numpy as jnp
import numpy as np
from jax import lax

D = 512
FF = 2048
NREL = 822
POS_WEIGHT = 64
NEG = 256
Q = 256
ROWS_DEV = 2048
CAP = 32
QUERIES = 8192
ROWS = 65536
N_ENT = 4
N_GRP = 8
DEVICES = 32


def plant(result, own_key, least, high):
    spot = [jax.random.randint(jax.random.fold_in(own_key, axis), (), 0, length) for axis, length in enumerate(result.shape)]
    widest = result.shape.index(max(result.shape))
    neighbour = spot[:widest] + [(spot[widest] + 1) % result.shape[widest]] + spot[widest + 1:]
    return result.at[tuple(spot)].set(least).at[tuple(neighbour)].set(high)


def level_of(key, shape, cuts, smallest, top_value):
    factor_of = 1.0
    for axis_at, blocks in cuts:
        heights = jax.random.uniform(jax.random.fold_in(jax.random.fold_in(key, 6), axis_at), (blocks,), jnp.float32, smallest / len(cuts), top_value / len(cuts))
        factor_of = factor_of * jnp.repeat(jnp.exp(heights), shape[axis_at] // blocks).reshape((-1,) + (1,) * (len(shape) - 1 - axis_at))
    return factor_of


def shared_out(rng, own, number, rows, number_of, top, most, skew):
    sequence = jax.random.permutation(rng, number_of)
    heavy_load, usual = load_shares(number_of, rows * top, most, skew, True), load_shares(number_of, rows * top, most, skew, False)
    places = jnp.arange(number_of)

    def named(tallies, turn):
        used = int((tallies > 0).sum())
        fixed = max(1, used // 4)
        moved = fixed + (places - fixed + turn * (used - fixed)) % max(1, number_of - fixed)
        return jnp.zeros((number_of,), jnp.int32).at[sequence[jnp.where(places < fixed, places, moved)]].set(jnp.asarray(tallies, jnp.int32))

    tallies = jnp.where(number % 4 == 0, named(heavy_load, number // 4), named(usual, number - number // 4 - 1))
    mixed = jax.random.permutation(jax.random.fold_in(own, 3), number_of)
    giver, sink = mixed[0:number_of // 2 * 2:2], mixed[1:number_of // 2 * 2:2]
    slack = jnp.minimum(tallies[giver] - 1, most - tallies[sink]) // 2
    slack = jnp.where((giver == sequence[0]) | (sink == sequence[0]) | (tallies[sink] == 0), 0, jnp.maximum(slack, 0))
    moved = jax.random.randint(jax.random.fold_in(own, 4), (number_of // 2,), 0, 1 << 20) % (slack + 1)
    tallies = tallies.at[giver].add(-moved).at[sink].add(moved)
    labels = jnp.searchsorted(jnp.cumsum(tallies), jnp.arange(rows * top), side="right").astype(jnp.int32)
    grid = labels.reshape(top, rows).T
    grid = grid[jax.random.permutation(jax.random.fold_in(own, 1), rows)]
    turn = jax.random.randint(jax.random.fold_in(own, 2), (rows, 1), 0, top)
    return jnp.take_along_axis(grid, (jnp.arange(top)[None, :] + turn) % top, axis=1)


def load_shares(count, total, most, slope, full):
    weights = [(1 << 20) // math.isqrt(standing ** slope) + 1 for standing in range(1, count + 1)]
    largest = most if full else min(most, max(-(-total // count), total * weights[0] // sum(weights)))
    least = 1 if total - largest >= count - 1 else 0
    counts, rest = [largest] + [least] * (count - 1), total - largest - least * (count - 1)
    while rest > 0:
        candidates = [i for i in range(1, count) if counts[i] < largest] or [i for i in range(1, count) if counts[i] < most]
        pool, remaining = sum([weights[i] for i in candidates]), rest
        for i in candidates:
            extra = min(most - counts[i], max(1, remaining * weights[i] // pool), rest)
            counts[i] = counts[i] + extra
            rest = rest - extra
    return np.array(counts)


def bell_draw(stream_key, dims, deviation, reach, cuts=(), kind=jnp.bfloat16):
    entries = deviation * jax.random.normal(stream_key, dims, jnp.float32)
    if cuts:
        entries = entries * level_of(stream_key, dims, cuts, -0.22, 0.18)
    return jnp.clip(entries, -reach, reach).astype(kind)


def setup_inputs(seed: int = 0) -> dict:
    key_list = jax.random.split(jax.random.key(seed), 12)
    table = bell_draw(key_list[0], (ROWS, D), 1.0, 6.0, ((0, 32),), jnp.float32)
    touch_owner_keys = jax.random.split(jax.random.fold_in(key_list[1], 1), (2 * QUERIES) // (2 * Q))
    touch_owner_turns = jax.random.permutation(jax.random.fold_in(key_list[1], 3), (2 * QUERIES) // (2 * Q))
    touch_owner = jax.vmap(lambda own, number: shared_out(jax.random.fold_in(key_list[1], 2), own, number, 2 * Q, DEVICES, 1, CAP, 2))(touch_owner_keys, touch_owner_turns).reshape((2 * QUERIES, 1))
    touch_local = plant(jax.random.randint(key_list[2], (2 * QUERIES,), 0, ROWS_DEV), jax.random.fold_in(key_list[2], 1), 0, ROWS_DEV - 1).astype(jnp.int32)
    query_rel = plant(jax.random.randint(key_list[3], (QUERIES,), 0, NREL), jax.random.fold_in(key_list[3], 1), 0, NREL - 1).astype(jnp.int32)
    neg_local = plant(jax.random.randint(key_list[4], (NEG * DEVICES,), 0, ROWS_DEV), jax.random.fold_in(key_list[4], 1), 0, ROWS_DEV - 1).astype(jnp.int32)
    rel_table = bell_draw(key_list[5], (NREL, D), 1.0, 6.0)
    in_gain = jnp.clip(1.0 + 0.18 * jax.random.normal(key_list[6], (D,), jnp.float32), 0.1, 1.9)
    out_gain = jnp.clip(1.0 + 0.18 * jax.random.normal(key_list[7], (D,), jnp.float32), 0.1, 1.9)
    w_gate = bell_draw(key_list[8], (D, FF), D ** -0.5, 0.25)
    w_up = bell_draw(key_list[9], (D, FF), D ** -0.5, 0.25)
    w_down = bell_draw(key_list[10], (FF, D), FF ** -0.5, 0.125)
    return dict(table=table, touch_owner=touch_owner, touch_local=touch_local, query_rel=query_rel, neg_local=neg_local, rel_table=rel_table, in_gain=in_gain, out_gain=out_gain, w_gate=w_gate, w_up=w_up, w_down=w_down)


norm_eps = 1e-06

def encode(head_rows, rel_rows, in_gain, out_gain, w_gate, w_up, w_down):
    base_sum = head_rows + rel_rows
    normed = (base_sum * lax.rsqrt(lax.optimization_barrier(jnp.mean(base_sum * base_sum, axis=-1, keepdims=True)) + norm_eps) * in_gain).astype(jnp.bfloat16)
    gate_proj = jnp.dot(normed, w_gate, preferred_element_type=jnp.float32)
    up_proj = jnp.dot(normed, w_up, preferred_element_type=jnp.float32)
    hidden = (jax.nn.silu(gate_proj) * up_proj).astype(jnp.bfloat16)
    mixed_sum = base_sum + jnp.dot(hidden, w_down, preferred_element_type=jnp.float32)
    return mixed_sum * lax.rsqrt(lax.optimization_barrier(jnp.mean(mixed_sum * mixed_sum, axis=-1, keepdims=True)) + norm_eps) * out_gain

def reference(table, touch_owner, touch_local, query_rel, neg_local, rel_table, in_gain, out_gain, w_gate, w_up, w_down):
    dev_count = N_ENT * N_GRP
    inv_scale = 1.0 / math.sqrt(D)
    row_ids = (touch_owner[:, 0].astype(jnp.int32) * ROWS_DEV + touch_local.astype(jnp.int32)).astype(jnp.int32)
    fetched = table[row_ids].astype(jnp.bfloat16).reshape(dev_count, 2, Q, D)
    head_rows = fetched[:, 0].reshape(N_ENT, N_GRP * Q, D)
    ctx_rows = fetched[:, 1].reshape(N_ENT, N_GRP * Q, D)
    rel_onehot = (query_rel[:, None] == jnp.arange(NREL, dtype=jnp.int32)[None, :]).astype(jnp.bfloat16)
    rel_rows = jnp.dot(rel_onehot, rel_table, preferred_element_type=jnp.float32).reshape(N_ENT, N_GRP * Q, D)
    neg_ids = (jnp.arange(dev_count, dtype=jnp.int32)[:, None] * ROWS_DEV + neg_local.astype(jnp.int32).reshape(dev_count, NEG)).astype(jnp.int32)
    negatives = table[neg_ids.reshape(-1)].astype(jnp.bfloat16).reshape(N_ENT, N_GRP * NEG, D)

    def per_group(operands):
        heads, contexts, relations, negs = operands

        def forward(head_f):
            return encode(head_f, relations, in_gain, out_gain, w_gate, w_up, w_down)
        query_vec, pullback = jax.vjp(forward, heads.astype(jnp.float32))
        query_bf = query_vec.astype(jnp.bfloat16)
        scores = jnp.dot(query_bf, negs.T, preferred_element_type=jnp.float32) * inv_scale
        neg_weight = (jax.nn.sigmoid(scores) * inv_scale).astype(jnp.bfloat16)
        ctx_f = contexts.astype(jnp.float32)
        pos_score = lax.optimization_barrier(jnp.sum(query_vec * ctx_f, axis=-1)) * inv_scale
        pos_weight = POS_WEIGHT * (jax.nn.sigmoid(pos_score) - 1.0) * inv_scale
        query_grad = jnp.dot(neg_weight, negs, preferred_element_type=jnp.float32) + pos_weight[:, None] * ctx_f
        ctx_grad = pos_weight[:, None] * query_vec
        head_grad = pullback(query_grad)[0]
        neg_grad = jnp.dot(neg_weight.T, query_bf, preferred_element_type=jnp.float32)
        return (head_grad, ctx_grad, neg_grad)
    head_grad, ctx_grad, neg_grad = lax.map(per_group, (head_rows, ctx_rows, rel_rows, negatives))
    ref_ids = row_ids.reshape(dev_count, 2, Q)
    table_grad = jnp.zeros((ROWS_DEV * dev_count, D), jnp.float32)
    table_grad = table_grad.at[ref_ids[:, 0].reshape(-1)].add(head_grad.reshape(-1, D))
    table_grad = table_grad.at[ref_ids[:, 1].reshape(-1)].add(ctx_grad.reshape(-1, D))
    table_grad = table_grad.at[neg_ids.reshape(-1)].add(neg_grad.reshape(-1, D))
    return table_grad
```

```python
import math

import jax
import jax.numpy as jnp
from jax import lax
from jax.sharding import PartitionSpec as P

POS_WEIGHT = 64


norm_eps = 1e-06


def encode(head_rows, rel_rows, in_gain, out_gain, w_gate, w_up, w_down):
    base_sum = head_rows + rel_rows
    normed = (
        base_sum
        * lax.rsqrt(jnp.mean(base_sum * base_sum, axis=-1, keepdims=True) + norm_eps)
        * in_gain
    ).astype(jnp.bfloat16)
    gate_proj = jnp.dot(normed, w_gate, preferred_element_type=jnp.float32)
    up_proj = jnp.dot(normed, w_up, preferred_element_type=jnp.float32)
    hidden = (jax.nn.silu(gate_proj) * up_proj).astype(jnp.bfloat16)
    mixed_sum = base_sum + jnp.dot(hidden, w_down, preferred_element_type=jnp.float32)
    return (
        mixed_sum
        * lax.rsqrt(jnp.mean(mixed_sum * mixed_sum, axis=-1, keepdims=True) + norm_eps)
        * out_gain
    )


def ring_order(count):
    inner = 1
    while inner * inner * 4 <= count and count % (inner * 2) == 0:
        inner *= 2
    outer = count // inner
    if inner == 1 or outer % 2:
        return list(range(count))
    walk = [row * inner for row in range(outer)]
    for back, row in enumerate(reversed(range(outer))):
        cols = range(1, inner) if back % 2 == 0 else reversed(range(1, inner))
        walk += [row * inner + col for col in cols]
    return walk


def ring_gather(block, axis):
    count = lax.axis_size(axis)
    walk = ring_order(count)
    ahead = [(walk[i], walk[(i + 1) % count]) for i in range(count)]
    behind = [(b, a) for a, b in ahead]
    pieces = [block]
    forth = back = block
    for _ in range((count - 1) // 2):
        forth = lax.ppermute(forth, axis, ahead)
        back = lax.ppermute(back, axis, behind)
        pieces += [forth, back]
    if count % 2 == 0:
        half = block.shape[0] // 2
        pieces.append(lax.ppermute(forth[:half], axis, ahead))
        pieces.append(lax.ppermute(back[half:], axis, behind))
    return pieces


def per_device(
    table,
    touch_owner,
    touch_local,
    query_rel,
    neg_local,
    rel_table,
    in_gain,
    out_gain,
    w_gate,
    w_up,
    w_down,
):
    ent_count = lax.axis_size("ent")
    grp_count = lax.axis_size("grp")
    dev_count = ent_count * grp_count
    ref_count = touch_local.shape[0]
    queries = ref_count // 2
    capacity = 2 * ref_count // dev_count
    feat_width = table.shape[1]
    inv_scale = 1.0 / math.sqrt(feat_width)
    owners = touch_owner[:, 0]
    owner_hits = (owners[:, None] == jnp.arange(dev_count, dtype=jnp.int32)[None, :]).astype(
        jnp.int32
    )
    placed = jnp.sum(jnp.cumsum(owner_hits, axis=0) * owner_hits, axis=1) - 1
    slot_index = owners * capacity + placed
    requests = (
        jnp.zeros((dev_count * capacity,), jnp.int32)
        .at[slot_index]
        .set(touch_local)
        .reshape(dev_count, capacity)
    )
    wanted = lax.all_to_all(requests, ("ent", "grp"), split_axis=0, concat_axis=0, tiled=True)
    looked = table[wanted.reshape(-1)].astype(jnp.bfloat16)
    fetched = lax.all_to_all(
        looked.reshape(wanted.shape + (feat_width,)),
        ("ent", "grp"),
        split_axis=0,
        concat_axis=0,
        tiled=True,
    )
    gathered = fetched.reshape(dev_count * capacity, feat_width)[slot_index]
    head_rows = gathered[:queries]
    ctx_rows = gathered[queries:]
    rel_onehot = (
        query_rel[:, None] == jnp.arange(rel_table.shape[0], dtype=jnp.int32)[None, :]
    ).astype(jnp.bfloat16)
    rel_rows = jnp.dot(rel_onehot, rel_table, preferred_element_type=jnp.float32)

    def forward(head_f):
        return encode(head_f, rel_rows, in_gain, out_gain, w_gate, w_up, w_down)

    query_vec, pullback = jax.vjp(forward, head_rows.astype(jnp.float32))
    query_bf = query_vec.astype(jnp.bfloat16)
    neg_rows = table[neg_local].astype(jnp.bfloat16)
    negatives = jnp.concatenate(ring_gather(neg_rows, "grp"))
    all_queries = jnp.concatenate(ring_gather(query_bf, "grp"))
    own_scores = jnp.dot(query_bf, negatives.T, preferred_element_type=jnp.float32) * inv_scale
    own_weight = (jax.nn.sigmoid(own_scores) * inv_scale).astype(jnp.bfloat16)
    neg_query_grad = jnp.dot(own_weight, negatives, preferred_element_type=jnp.float32)
    group_scores = jnp.dot(all_queries, neg_rows.T, preferred_element_type=jnp.float32) * inv_scale
    group_weight = (jax.nn.sigmoid(group_scores) * inv_scale).astype(jnp.bfloat16)
    neg_grad = jnp.dot(group_weight.T, all_queries, preferred_element_type=jnp.float32)
    ctx_f = ctx_rows.astype(jnp.float32)
    pos_score = jnp.sum(query_vec * ctx_f, axis=-1) * inv_scale
    pos_weight = POS_WEIGHT * (jax.nn.sigmoid(pos_score) - 1.0) * inv_scale
    query_grad = neg_query_grad + pos_weight[:, None] * ctx_f
    ctx_grad = pos_weight[:, None] * query_vec
    head_grad = pullback(query_grad)[0]
    ref_grads = jnp.concatenate([head_grad, ctx_grad], axis=0)
    outgoing = (
        jnp.zeros((dev_count * capacity, feat_width), jnp.bfloat16)
        .at[slot_index]
        .set(ref_grads.astype(jnp.bfloat16))
    )
    returned = lax.all_to_all(
        outgoing.reshape(dev_count, capacity, feat_width),
        ("ent", "grp"),
        split_axis=0,
        concat_axis=0,
        tiled=True,
    )
    table_grad = jnp.zeros(table.shape, jnp.float32)
    table_grad = table_grad.at[wanted.reshape(-1)].add(
        returned.reshape(-1, feat_width).astype(jnp.float32)
    )
    table_grad = table_grad.at[neg_local].add(neg_grad)
    return table_grad


def solution(mesh):
    return jax.shard_map(
        per_device,
        mesh=mesh,
        in_specs=(
            P(("ent", "grp"), None),
            P(("ent", "grp"), None),
            P(("ent", "grp")),
            P(("ent", "grp")),
            P(("ent", "grp")),
            P(),
            P(),
            P(),
            P(),
            P(),
            P(),
        ),
        out_specs=P(("ent", "grp"), None),
        check_vma=False,
    )
```

```python
import functools
import math

import jax
import jax.numpy as jnp
from jax import lax
from jax.experimental import pallas as pl
from jax.experimental.pallas import tpu as pltpu
from jax.sharding import PartitionSpec as P

POS_WEIGHT = 64

norm_eps = 1e-06

F32 = jnp.float32
BF16 = jnp.bfloat16
I32 = jnp.int32
MIB = 1 << 20

NN = (((1,), (0,)), ((), ()))
NT = (((1,), (1,)), ((), ()))
TN = (((0,), (0,)), ((), ()))


def dot(a, b, dims=NN):
    return lax.dot_general(a, b, dims, preferred_element_type=F32)


def iota(shape, axis):
    return lax.broadcasted_iota(I32, shape, axis)


def ones_where(mask):
    return jnp.where(mask, 1.0, 0.0).astype(BF16)


def to_column(row):
    count = row.shape[1]
    same = iota((count, count), 0) == iota((count, count), 1)
    return jnp.sum(jnp.where(same, row, 0.0), axis=1, keepdims=True)


def to_row(column):
    count = column.shape[0]
    same = iota((count, count), 0) == iota((count, count), 1)
    return jnp.sum(jnp.where(same, column, 0.0), axis=0, keepdims=True)


def split_bytes(numbers):
    high = jnp.floor(numbers * (1.0 / 256.0))
    return high.astype(BF16), (numbers - high * 256.0).astype(BF16)


def call(kernel, out_shape, args, flops, moved, **kwargs):
    return pl.pallas_call(
        kernel,
        out_shape=out_shape,
        compiler_params=pltpu.CompilerParams(vmem_limit_bytes=kwargs.pop("vmem", 28 * MIB)),
        cost_estimate=pl.CostEstimate(flops=flops, bytes_accessed=moved, transcendentals=0),
        **kwargs,
    )(*args)


def route_kernel(owner_ref, local_ref, request_ref, slot_col_ref, slot_row_ref):
    refs = owner_ref.shape[0]
    dev_count, capacity = request_ref.shape
    owner = owner_ref[...]
    hit = owner == iota((refs, dev_count), 1)
    hit_one = ones_where(hit)
    earlier = ones_where(iota((refs, refs), 1) <= iota((refs, refs), 0))
    rank = dot(earlier, hit_one)
    placed = jnp.sum(jnp.where(hit, rank, 0.0), axis=1, keepdims=True) - 1.0
    slot = owner.astype(F32) * float(capacity) + placed
    local = to_column(local_ref[...].astype(F32))
    at = placed.astype(I32) == iota((refs, capacity), 1)
    high, low = split_bytes(jnp.where(at, local, 0.0))
    request = dot(hit_one, high, TN) * 256.0 + dot(hit_one, low, TN)
    request_ref[...] = request.astype(I32)
    slot_col_ref[...] = slot.astype(I32)
    slot_row_ref[...] = to_row(slot).astype(I32)


def negatives_kernel(local_ref, table_ref, neg_ref, small_ref, sum_ref):
    step = pl.program_id(0)
    rows = table_ref.shape[0]
    small = table_ref[...].astype(BF16)
    small_ref[...] = small
    local = to_column(local_ref[...].astype(F32)).astype(I32) - step * rows
    picked = dot(ones_where(local == iota((neg_ref.shape[0], rows), 1)), small)

    @pl.when(step == 0)
    def _():
        sum_ref[...] = picked

    @pl.when(step > 0)
    def _():
        sum_ref[...] += picked

    @pl.when(step == pl.num_programs(0) - 1)
    def _():
        neg_ref[...] = sum_ref[...].astype(BF16)


def wanted_parts(wanted_ref):
    high, low = split_bytes(wanted_ref[...].astype(F32))
    return high, low


def fetch_kernel(wanted_ref, table_ref, out_ref):
    dev_count, capacity = wanted_ref.shape
    slots = out_ref.shape[0]
    rows = table_ref.shape[0]
    high, low = split_bytes(wanted_ref[...].astype(F32))
    first = iota((slots, dev_count), 1) * capacity
    slot = iota((slots, dev_count), 0)
    mine = ones_where((slot >= first) & (slot < first + capacity))
    spread = dot(mine, high) * 256.0 + dot(mine, low)
    at = lax.rem(iota((slots, capacity), 0), capacity) == iota((slots, capacity), 1)
    wanted = jnp.sum(jnp.where(at, spread, 0.0), axis=1, keepdims=True).astype(I32)
    block = math.gcd(slots, 256)
    for start in range(0, slots, block):
        hot = ones_where(wanted[start : start + block] == iota((block, rows), 1))
        out_ref[start : start + block, :] = dot(hot, table_ref[...]).astype(BF16)


def encode_kernel(
    fetched_ref,
    slot_ref,
    rel_ref,
    in_gain_ref,
    out_gain_ref,
    gate_ref,
    up_ref,
    down_ref,
    query_bf_ref,
    query_ref,
    base_ref,
    ctx_ref,
    mixed_ref,
    silu_ref,
    slope_ref,
):
    queries = rel_ref.shape[0]
    refs = slot_ref.shape[0]
    slots = fetched_ref.shape[0]
    pick = ones_where(slot_ref[...] == iota((refs, slots), 1))
    gathered = dot(pick, fetched_ref[...])
    ctx_ref[...] = gathered[queries:].astype(BF16)
    base = gathered[:queries] + rel_ref[...]
    base_ref[...] = base
    in_scale = lax.rsqrt(jnp.mean(base * base, axis=-1, keepdims=True) + norm_eps)
    normed = (base * in_scale * in_gain_ref[...]).astype(BF16)
    gate = dot(normed, gate_ref[...])
    up = dot(normed, up_ref[...])
    sig = jax.nn.sigmoid(gate)
    silu = gate * sig
    hidden = (silu * up).astype(BF16)
    silu_ref[...] = silu.astype(BF16)
    slope_ref[...] = (up * (sig + silu * (1.0 - sig))).astype(BF16)
    mixed = base + dot(hidden, down_ref[...])
    mixed_ref[...] = mixed
    out_scale = lax.rsqrt(jnp.mean(mixed * mixed, axis=-1, keepdims=True) + norm_eps)
    query = mixed * out_scale * out_gain_ref[...]
    query_ref[...] = query
    query_bf_ref[...] = query.astype(BF16)


def norm_pull(value, gain, cotangent):
    scale = lax.rsqrt(jnp.mean(value * value, axis=-1, keepdims=True) + norm_eps)
    scaled = cotangent * gain
    along = jnp.mean(scaled * value, axis=-1, keepdims=True)
    return scale * scaled - value * (along * scale * scale * scale)


def grad_kernel(inv_scale, pieces, *refs):
    neg_refs = refs[:pieces]
    (
        query_bf_ref,
        query_ref,
        base_ref,
        ctx_ref,
        mixed_ref,
        silu_ref,
        slope_ref,
        slot_ref,
        in_gain_ref,
        out_gain_ref,
        gate_ref,
        up_ref,
        down_ref,
        out_ref,
    ) = refs[pieces:]
    query_bf = query_bf_ref[...]
    query = query_ref[...]
    ctx = ctx_ref[...].astype(F32)
    pos_score = jnp.sum(query * ctx, axis=-1, keepdims=True) * inv_scale
    pos_weight = POS_WEIGHT * (jax.nn.sigmoid(pos_score) - 1.0) * inv_scale
    query_grad = pos_weight * ctx
    for neg_ref in neg_refs:
        neg = neg_ref[...]
        scores = dot(query_bf, neg, NT) * inv_scale
        weight = (jax.nn.sigmoid(scores) * inv_scale).astype(BF16)
        query_grad = query_grad + dot(weight, neg)
    ctx_grad = pos_weight * query
    mixed_cot = norm_pull(mixed_ref[...], out_gain_ref[...], query_grad)
    hidden_cot = dot(mixed_cot.astype(BF16), down_ref[...], NT).astype(BF16).astype(F32)
    gate_cot = (hidden_cot * slope_ref[...].astype(F32)).astype(BF16)
    up_cot = (hidden_cot * silu_ref[...].astype(F32)).astype(BF16)
    normed_cot = dot(gate_cot, gate_ref[...], NT) + dot(up_cot, up_ref[...], NT)
    normed_cot = normed_cot.astype(BF16).astype(F32)
    head_grad = mixed_cot + norm_pull(base_ref[...], in_gain_ref[...], normed_cot)
    slots = out_ref.shape[0]
    queries = query.shape[0]
    slot = slot_ref[...]
    place = ones_where(iota((slots, slot.shape[1]), 0) == slot)
    out = dot(place[:, :queries], head_grad.astype(BF16)) + dot(
        place[:, queries:], ctx_grad.astype(BF16)
    )
    out_ref[...] = out.astype(BF16)


def neg_grad_kernel(inv_scale, pieces, *refs):
    query_refs = refs[:pieces]
    neg_ref, high_ref, low_ref = refs[pieces:]
    neg = neg_ref[...]
    total = jnp.zeros(neg.shape, F32)
    for query_ref in query_refs:
        query = query_ref[...]
        scores = dot(neg, query, NT) * inv_scale
        weight = (jax.nn.sigmoid(scores) * inv_scale).astype(BF16)
        total = total + dot(weight, query)
    high = total.astype(BF16)
    high_ref[...] = high
    low_ref[...] = (total - high.astype(F32)).astype(BF16)


def scatter_kernel(wanted_ref, local_ref, back_ref, high_ref, low_ref, out_ref):
    dev_count, capacity = wanted_ref.shape
    slots = back_ref.shape[0]
    rows = out_ref.shape[0]
    high, low = split_bytes(wanted_ref[...].astype(F32))
    at = ones_where(
        lax.rem(iota((capacity, slots), 1), capacity) == iota((capacity, slots), 0)
    )
    spread = dot(high, at) * 256.0 + dot(low, at)
    first = iota((dev_count, slots), 0) * capacity
    slot = iota((dev_count, slots), 1)
    mine = (slot >= first) & (slot < first + capacity)
    wanted = jnp.sum(jnp.where(mine, spread, 0.0), axis=0, keepdims=True).astype(I32)
    start = pl.program_id(0) * rows
    place = ones_where(iota((rows, slots), 0) + start == wanted)
    local = local_ref[...]
    spot = ones_where(iota((rows, local.shape[1]), 0) + start == local)
    out_ref[...] = (
        dot(place, back_ref[...]) + dot(spot, high_ref[...]) + dot(spot, low_ref[...])
    )


def group_pieces(block, axis):
    count = lax.axis_size(axis)
    if count & (count - 1):
        return [lax.all_gather(block, axis, axis=0, tiled=True)]
    held = {0: block}
    for bits in range(1, count.bit_length()):
        for other in range(1, count):
            if bin(other).count("1") == bits:
                step = other & -other
                held[other] = lax.ppermute(
                    held[other - step], axis, [(i, i ^ step) for i in range(count)]
                )
    return [held[other] for other in range(count)]


def per_device(
    table,
    touch_owner,
    touch_local,
    query_rel,
    neg_local,
    rel_table,
    in_gain,
    out_gain,
    w_gate,
    w_up,
    w_down,
):
    axes = ("ent", "grp")
    dev_count = lax.axis_size("ent") * lax.axis_size("grp")
    refs = touch_local.shape[0]
    queries = refs // 2
    capacity = 2 * refs // dev_count
    slots = dev_count * capacity
    rows, width = table.shape
    hidden = w_gate.shape[1]
    negs = neg_local.shape[0]
    inv_scale = 1.0 / math.sqrt(width)
    shape = jax.ShapeDtypeStruct
    in_gain = in_gain.reshape(1, width)
    out_gain = out_gain.reshape(1, width)
    neg_row = neg_local.reshape(1, negs)

    requests, slot_col, slot_row = call(
        route_kernel,
        (shape((dev_count, capacity), I32), shape((refs, 1), I32), shape((1, refs), I32)),
        (touch_owner, touch_local.reshape(1, refs)),
        2 * refs * refs * dev_count,
        4 * refs * 130,
    )
    wanted = lax.all_to_all(requests, axes, split_axis=0, concat_axis=0, tiled=True)

    steps = 4 if rows % 64 == 0 else 1
    neg_rows, small_table = call(
        negatives_kernel,
        (shape((negs, width), BF16), shape((rows, width), BF16)),
        (neg_row, table),
        2 * negs * rows * width,
        6 * rows * width,
        grid=(steps,),
        in_specs=[
            pl.BlockSpec((1, negs), lambda i: (0, 0)),
            pl.BlockSpec((rows // steps, width), lambda i: (i, 0)),
        ],
        out_specs=(
            pl.BlockSpec((negs, width), lambda i: (0, 0)),
            pl.BlockSpec((rows // steps, width), lambda i: (i, 0)),
        ),
        scratch_shapes=[pltpu.VMEM((negs, width), F32)],
    )
    neg_pieces = group_pieces(neg_rows, "grp")

    looked = call(
        fetch_kernel,
        shape((slots, width), BF16),
        (wanted, small_table),
        2 * slots * rows * width,
        2 * (slots + rows) * width,
    )
    fetched = lax.all_to_all(
        looked.reshape(dev_count, capacity, width), axes, split_axis=0, concat_axis=0, tiled=True
    ).reshape(slots, width)

    rel_onehot = (
        query_rel[:, None] == jnp.arange(rel_table.shape[0], dtype=jnp.int32)[None, :]
    ).astype(BF16)
    rel_rows = jnp.dot(rel_onehot, rel_table, preferred_element_type=F32)

    query_bf, query, base, ctx, mixed, silu, slope = call(
        encode_kernel,
        (
            shape((queries, width), BF16),
            shape((queries, width), F32),
            shape((queries, width), F32),
            shape((queries, width), BF16),
            shape((queries, width), F32),
            shape((queries, hidden), BF16),
            shape((queries, hidden), BF16),
        ),
        (fetched, slot_col, rel_rows, in_gain, out_gain, w_gate, w_up, w_down),
        2 * queries * width * (2 * slots + 3 * hidden),
        2 * (slots * width + 3 * width * hidden),
    )
    query_pieces = group_pieces(query_bf, "grp")

    outgoing = call(
        functools.partial(grad_kernel, inv_scale, len(neg_pieces)),
        shape((slots, width), BF16),
        (
            *neg_pieces,
            query_bf,
            query,
            base,
            ctx,
            mixed,
            silu,
            slope,
            slot_row,
            in_gain,
            out_gain,
            w_gate,
            w_up,
            w_down,
        ),
        2 * queries * width * (2 * slots + 3 * hidden + 2 * negs * len(neg_pieces)),
        2 * (slots * width + 3 * width * hidden + negs * width * len(neg_pieces)),
    )
    returned = lax.all_to_all(
        outgoing.reshape(dev_count, capacity, width), axes, split_axis=0, concat_axis=0, tiled=True
    ).reshape(slots, width)

    neg_high, neg_low = call(
        functools.partial(neg_grad_kernel, inv_scale, len(query_pieces)),
        (shape((negs, width), BF16), shape((negs, width), BF16)),
        (*query_pieces, neg_rows),
        4 * queries * negs * width * len(query_pieces),
        2 * queries * width * len(query_pieces),
    )

    blocks = 8 if rows % 128 == 0 else 1
    whole = lambda a: pl.BlockSpec(a.shape, lambda i: (0, 0))
    operands = (wanted, neg_row, returned, neg_high, neg_low)
    return call(
        scatter_kernel,
        shape((rows, width), F32),
        operands,
        2 * rows * width * (slots + 2 * negs),
        4 * rows * width + 2 * slots * width,
        grid=(blocks,),
        in_specs=[whole(a) for a in operands],
        out_specs=pl.BlockSpec((rows // blocks, width), lambda i: (i, 0)),
    )


def solution(mesh):
    return jax.shard_map(
        per_device,
        mesh=mesh,
        in_specs=(
            P(("ent", "grp"), None),
            P(("ent", "grp"), None),
            P(("ent", "grp")),
            P(("ent", "grp")),
            P(("ent", "grp")),
            P(),
            P(),
            P(),
            P(),
            P(),
            P(),
        ),
        out_specs=P(("ent", "grp"), None),
        check_vma=False,
    )
```

```python
import functools
import math

import jax
import jax.numpy as jnp
from jax import lax
from jax.experimental import pallas as pl
from jax.experimental.pallas import tpu as pltpu
from jax.sharding import PartitionSpec as P

POS_WEIGHT = 64

norm_eps = 1e-06

F32 = jnp.float32
BF16 = jnp.bfloat16
I32 = jnp.int32
MIB = 1 << 20

NN = (((1,), (0,)), ((), ()))
NT = (((1,), (1,)), ((), ()))
TN = (((0,), (0,)), ((), ()))


def dot(a, b, dims=NN):
    return lax.dot_general(a, b, dims, preferred_element_type=F32)


def iota(shape, axis):
    return lax.broadcasted_iota(I32, shape, axis)


def ones_where(mask):
    return jnp.where(mask, 1.0, 0.0).astype(BF16)


def to_column(row):
    count = row.shape[1]
    same = iota((count, count), 0) == iota((count, count), 1)
    return jnp.sum(jnp.where(same, row, 0.0), axis=1, keepdims=True)


def to_row(column):
    count = column.shape[0]
    same = iota((count, count), 0) == iota((count, count), 1)
    return jnp.sum(jnp.where(same, column, 0.0), axis=0, keepdims=True)


def split_bytes(numbers):
    high = jnp.floor(numbers * (1.0 / 256.0))
    return high.astype(BF16), (numbers - high * 256.0).astype(BF16)


def call(kernel, out_shape, args, flops, moved, **kwargs):
    return pl.pallas_call(
        kernel,
        out_shape=out_shape,
        compiler_params=pltpu.CompilerParams(vmem_limit_bytes=kwargs.pop("vmem", 28 * MIB)),
        cost_estimate=pl.CostEstimate(flops=flops, bytes_accessed=moved, transcendentals=0),
        **kwargs,
    )(*args)


def prepare_kernel(
    owner_ref,
    local_ref,
    neg_local_ref,
    table_ref,
    request_ref,
    slot_row_ref,
    neg_ref,
    small_ref,
    stage_ref,
    sem,
):
    parts, rows, _ = stage_ref.shape
    copies = [
        pltpu.make_async_copy(
            table_ref.at[pl.ds(part * rows, rows)], stage_ref.at[part], sem.at[part]
        )
        for part in range(parts)
    ]
    for copy in copies:
        copy.start()
    refs = owner_ref.shape[1]
    dev_count, capacity = request_ref.shape
    owner = to_column(owner_ref[...].astype(F32))
    hit = owner.astype(I32) == iota((refs, dev_count), 1)
    hit_one = ones_where(hit)
    earlier = ones_where(iota((refs, refs), 1) <= iota((refs, refs), 0))
    rank = dot(earlier, hit_one)
    placed = jnp.sum(jnp.where(hit, rank, 0.0), axis=1, keepdims=True) - 1.0
    slot = owner * float(capacity) + placed
    local = to_column(local_ref[...].astype(F32))
    at = placed.astype(I32) == iota((refs, capacity), 1)
    high, low = split_bytes(jnp.where(at, local, 0.0))
    request = dot(hit_one, high, TN) * 256.0 + dot(hit_one, low, TN)
    request_ref[...] = request.astype(I32)
    slot_row_ref[...] = to_row(slot).astype(I32)
    neg_local = to_column(neg_local_ref[...].astype(F32)).astype(I32)
    total = jnp.zeros(neg_ref.shape, F32)
    for part, copy in enumerate(copies):
        copy.wait()
        small = stage_ref[part].astype(BF16)
        small_ref[part * rows : (part + 1) * rows, :] = small
        hot = neg_local == iota((neg_ref.shape[0], rows), 1) + part * rows
        total = total + dot(ones_where(hot), small)
    neg_ref[...] = total.astype(BF16)


def fetch_kernel(pieces, *refs):
    wanted_ref, table_ref, out_ref = refs[pieces:]
    dev_count, capacity = wanted_ref.shape
    slots = out_ref.shape[0]
    rows = table_ref.shape[0]
    high, low = split_bytes(wanted_ref[...].astype(F32))
    first = iota((slots, dev_count), 1) * capacity
    slot = iota((slots, dev_count), 0)
    mine = ones_where((slot >= first) & (slot < first + capacity))
    spread = dot(mine, high) * 256.0 + dot(mine, low)
    at = lax.rem(iota((slots, capacity), 0), capacity) == iota((slots, capacity), 1)
    wanted = jnp.sum(jnp.where(at, spread, 0.0), axis=1, keepdims=True).astype(I32)
    block = math.gcd(slots, 256)
    for start in range(0, slots, block):
        hot = ones_where(wanted[start : start + block] == iota((block, rows), 1))
        out_ref[start : start + block, :] = dot(hot, table_ref[...]).astype(BF16)


def load_weights(sources, buffers, sem):
    copies = [
        pltpu.make_async_copy(source, buffer, sem.at[i])
        for i, (source, buffer) in enumerate(zip(sources, buffers))
    ]
    for copy in copies:
        copy.start()
    return copies


def encode_kernel(
    fetched_ref,
    slot_ref,
    rel_ref,
    in_gain_ref,
    out_gain_ref,
    gate_ref,
    up_ref,
    down_ref,
    query_bf_ref,
    query_ref,
    base_ref,
    ctx_ref,
    mixed_ref,
    silu_ref,
    slope_ref,
    gate_buf,
    up_buf,
    down_buf,
    sem,
):
    loads = load_weights((gate_ref, up_ref, down_ref), (gate_buf, up_buf, down_buf), sem)
    queries = rel_ref.shape[0]
    refs = slot_ref.shape[1]
    slots = fetched_ref.shape[0]
    slot = to_column(slot_ref[...].astype(F32)).astype(I32)
    pick = ones_where(slot == iota((refs, slots), 1))
    gathered = dot(pick, fetched_ref[...])
    ctx_ref[...] = gathered[queries:].astype(BF16)
    base = gathered[:queries] + rel_ref[...]
    base_ref[...] = base
    in_scale = lax.rsqrt(jnp.mean(base * base, axis=-1, keepdims=True) + norm_eps)
    normed = (base * in_scale * in_gain_ref[...]).astype(BF16)
    loads[0].wait()
    gate = dot(normed, gate_buf[...])
    loads[1].wait()
    up = dot(normed, up_buf[...])
    sig = jax.nn.sigmoid(gate)
    silu = gate * sig
    hidden = (silu * up).astype(BF16)
    silu_ref[...] = silu.astype(BF16)
    slope_ref[...] = (up * (sig + silu * (1.0 - sig))).astype(BF16)
    loads[2].wait()
    mixed = base + dot(hidden, down_buf[...])
    mixed_ref[...] = mixed
    out_scale = lax.rsqrt(jnp.mean(mixed * mixed, axis=-1, keepdims=True) + norm_eps)
    query = mixed * out_scale * out_gain_ref[...]
    query_ref[...] = query
    query_bf_ref[...] = query.astype(BF16)


def norm_pull(value, gain, cotangent):
    scale = lax.rsqrt(jnp.mean(value * value, axis=-1, keepdims=True) + norm_eps)
    scaled = cotangent * gain
    along = jnp.mean(scaled * value, axis=-1, keepdims=True)
    return scale * scaled - value * (along * scale * scale * scale)


def grad_kernel(inv_scale, pieces, *refs):
    neg_refs = refs[:pieces]
    (
        query_bf_ref,
        query_ref,
        base_ref,
        ctx_ref,
        mixed_ref,
        silu_ref,
        slope_ref,
        slot_ref,
        in_gain_ref,
        out_gain_ref,
        gate_ref,
        up_ref,
        down_ref,
        out_ref,
        gate_buf,
        up_buf,
        down_buf,
        sem,
    ) = refs[pieces:]
    loads = load_weights((down_ref, gate_ref, up_ref), (down_buf, gate_buf, up_buf), sem)
    query_bf = query_bf_ref[...]
    query = query_ref[...]
    ctx = ctx_ref[...].astype(F32)
    pos_score = jnp.sum(query * ctx, axis=-1, keepdims=True) * inv_scale
    pos_weight = POS_WEIGHT * (jax.nn.sigmoid(pos_score) - 1.0) * inv_scale
    query_grad = pos_weight * ctx
    for neg_ref in neg_refs:
        neg = neg_ref[...]
        scores = dot(query_bf, neg, NT) * inv_scale
        weight = (jax.nn.sigmoid(scores) * inv_scale).astype(BF16)
        query_grad = query_grad + dot(weight, neg)
    ctx_grad = pos_weight * query
    mixed_cot = norm_pull(mixed_ref[...], out_gain_ref[...], query_grad)
    loads[0].wait()
    hidden_cot = dot(mixed_cot.astype(BF16), down_buf[...], NT).astype(BF16).astype(F32)
    gate_cot = (hidden_cot * slope_ref[...].astype(F32)).astype(BF16)
    up_cot = (hidden_cot * silu_ref[...].astype(F32)).astype(BF16)
    loads[1].wait()
    normed_cot = dot(gate_cot, gate_buf[...], NT)
    loads[2].wait()
    normed_cot = normed_cot + dot(up_cot, up_buf[...], NT)
    normed_cot = normed_cot.astype(BF16).astype(F32)
    head_grad = mixed_cot + norm_pull(base_ref[...], in_gain_ref[...], normed_cot)
    slots = out_ref.shape[0]
    queries = query.shape[0]
    slot = slot_ref[...]
    place = ones_where(iota((slots, slot.shape[1]), 0) == slot)
    out = dot(place[:, :queries], head_grad.astype(BF16)) + dot(
        place[:, queries:], ctx_grad.astype(BF16)
    )
    out_ref[...] = out.astype(BF16)


def neg_grad_kernel(inv_scale, pieces, *refs):
    query_refs = refs[:pieces]
    neg_ref, out_ref = refs[pieces:]
    neg = neg_ref[...]
    total = jnp.zeros(neg.shape, F32)
    for query_ref in query_refs:
        query = query_ref[...]
        scores = dot(neg, query, NT) * inv_scale
        weight = (jax.nn.sigmoid(scores) * inv_scale).astype(BF16)
        total = total + dot(weight, query)
    out_ref[...] = total.astype(out_ref.dtype)


def wanted_row_kernel(wanted_ref, out_ref):
    dev_count, capacity = wanted_ref.shape
    slots = out_ref.shape[1]
    high, low = split_bytes(wanted_ref[...].astype(F32))
    at = ones_where(
        lax.rem(iota((capacity, slots), 1), capacity) == iota((capacity, slots), 0)
    )
    spread = dot(high, at) * 256.0 + dot(low, at)
    first = iota((dev_count, slots), 0) * capacity
    slot = iota((dev_count, slots), 1)
    mine = (slot >= first) & (slot < first + capacity)
    out_ref[...] = jnp.sum(jnp.where(mine, spread, 0.0), axis=0, keepdims=True).astype(I32)


def scatter_kernel(parts, *refs):
    sent_refs = refs[:parts]
    wanted_ref, local_ref, back_ref, own_ref, out_ref, neg_ref = refs[parts:]
    slots = back_ref.shape[0]
    rows = out_ref.shape[0]

    @pl.when(pl.program_id(0) == 0)
    def _():
        total = own_ref[...]
        for sent_ref in sent_refs:
            total = total + sent_ref[...].astype(F32)
        neg_ref[...] = total.astype(BF16)

    start = pl.program_id(0) * rows
    place = ones_where(iota((rows, slots), 0) + start == wanted_ref[...])
    local = local_ref[...]
    spot = ones_where(iota((rows, local.shape[1]), 0) + start == local)
    out_ref[...] = dot(place, back_ref[...]) + dot(spot, neg_ref[...])


def grid_inner(count):
    return 1 << ((count.bit_length() - 1) // 2)


def flip(block, axis, step):
    count = lax.axis_size(axis)
    return lax.ppermute(block, axis, [(i, i ^ step) for i in range(count)])


def spread_over(block, axis, others):
    held = {0: block}
    for other in sorted(others, key=lambda n: (bin(n).count("1"), -n)):
        step = other & -other
        held[other] = flip(held[other - step], axis, step)
    return held


def per_device(
    table,
    touch_owner,
    touch_local,
    query_rel,
    neg_local,
    rel_table,
    in_gain,
    out_gain,
    w_gate,
    w_up,
    w_down,
):
    axes = ("ent", "grp")
    dev_count = lax.axis_size("ent") * lax.axis_size("grp")
    refs = touch_local.shape[0]
    queries = refs // 2
    capacity = 2 * refs // dev_count
    slots = dev_count * capacity
    rows, width = table.shape
    hidden = w_gate.shape[1]
    negs = neg_local.shape[0]
    inv_scale = 1.0 / math.sqrt(width)
    shape = jax.ShapeDtypeStruct
    in_gain = in_gain.reshape(1, width)
    out_gain = out_gain.reshape(1, width)
    neg_row = neg_local.reshape(1, negs)

    group = lax.axis_size("grp")
    inner = grid_inner(group)
    hbm = pl.BlockSpec(memory_space=pltpu.HBM)
    vmem = pl.BlockSpec(memory_space=pltpu.VMEM)

    parts = 4 if rows % 64 == 0 else 1
    requests, slot_row, neg_rows, small_table = call(
        prepare_kernel,
        (
            shape((dev_count, capacity), I32),
            shape((1, refs), I32),
            shape((negs, width), BF16),
            shape((rows, width), BF16),
        ),
        (touch_owner.reshape(1, refs), touch_local.reshape(1, refs), neg_row, table),
        2 * negs * rows * width,
        6 * rows * width,
        in_specs=[vmem, vmem, vmem, hbm],
        scratch_shapes=[
            pltpu.VMEM((parts, rows // parts, width), F32),
            pltpu.SemaphoreType.DMA((parts,)),
        ],
    )
    neg_held = spread_over(neg_rows, "grp", range(1, group))
    neg_pieces = [neg_held[other] for other in range(group)]
    wanted = lax.all_to_all(requests, axes, split_axis=0, concat_axis=0, tiled=True)

    ahead = [neg_held[1 << bit] for bit in range(group.bit_length() - 1)]
    looked = call(
        functools.partial(fetch_kernel, len(ahead)),
        shape((slots, width), BF16),
        (*ahead, wanted, small_table),
        2 * slots * rows * width,
        2 * (slots + rows) * width,
        in_specs=[pl.BlockSpec(memory_space=pl.ANY)] * len(ahead) + [vmem, vmem],
    )
    fetched = lax.all_to_all(
        looked.reshape(dev_count, capacity, width), axes, split_axis=0, concat_axis=0, tiled=True
    ).reshape(slots, width)

    rel_onehot = (
        query_rel[:, None] == jnp.arange(rel_table.shape[0], dtype=jnp.int32)[None, :]
    ).astype(BF16)
    rel_rows = jnp.dot(rel_onehot, rel_table, preferred_element_type=F32)

    weight_scratch = [
        pltpu.VMEM(w_gate.shape, BF16),
        pltpu.VMEM(w_up.shape, BF16),
        pltpu.VMEM(w_down.shape, BF16),
        pltpu.SemaphoreType.DMA((3,)),
    ]
    query_bf, query, base, ctx, mixed, silu, slope = call(
        encode_kernel,
        (
            shape((queries, width), BF16),
            shape((queries, width), F32),
            shape((queries, width), F32),
            shape((queries, width), BF16),
            shape((queries, width), F32),
            shape((queries, hidden), BF16),
            shape((queries, hidden), BF16),
        ),
        (fetched, slot_row, rel_rows, in_gain, out_gain, w_gate, w_up, w_down),
        2 * queries * width * (2 * slots + 3 * hidden),
        2 * (slots * width + 3 * width * hidden),
        in_specs=[vmem] * 5 + [hbm] * 3,
        scratch_shapes=weight_scratch,
    )
    query_held = spread_over(query_bf, "grp", range(inner, group, inner))
    query_pieces = list(query_held.values())

    outgoing = call(
        functools.partial(grad_kernel, inv_scale, len(neg_pieces)),
        shape((slots, width), BF16),
        (
            *neg_pieces,
            query_bf,
            query,
            base,
            ctx,
            mixed,
            silu,
            slope,
            slot_row,
            in_gain,
            out_gain,
            w_gate,
            w_up,
            w_down,
        ),
        2 * queries * width * (2 * slots + 3 * hidden + 2 * negs * len(neg_pieces)),
        2 * (slots * width + 3 * width * hidden + negs * width * len(neg_pieces)),
        in_specs=[vmem] * (len(neg_pieces) + 10) + [hbm] * 3,
        scratch_shapes=weight_scratch,
    )
    if group > inner:
        outgoing, query_held[group // 2] = lax.optimization_barrier(
            (outgoing, query_held[group // 2])
        )
    returned = lax.all_to_all(
        outgoing.reshape(dev_count, capacity, width), axes, split_axis=0, concat_axis=0, tiled=True
    ).reshape(slots, width)

    def neg_grad(other, dtype):
        return call(
            functools.partial(neg_grad_kernel, inv_scale, len(query_pieces)),
            shape((negs, width), dtype),
            (*query_pieces, neg_held[other]),
            4 * queries * negs * width * len(query_pieces),
            2 * queries * width * len(query_pieces),
        )

    sent = [flip(neg_grad(other, BF16), "grp", other) for other in range(1, inner)]
    own = neg_grad(0, F32)
    wanted_row = call(
        wanted_row_kernel, shape((1, slots), I32), (wanted,), slots * dev_count, 4 * slots
    )

    blocks = 4 if rows % 64 == 0 else 1
    whole = lambda a: pl.BlockSpec(a.shape, lambda i: (0, 0))
    operands = (*sent, wanted_row, neg_row, returned, own)
    return call(
        functools.partial(scatter_kernel, len(sent)),
        shape((rows, width), F32),
        operands,
        2 * rows * width * (slots + negs),
        4 * rows * width + 2 * slots * width,
        grid=(blocks,),
        in_specs=[whole(a) for a in operands],
        out_specs=pl.BlockSpec((rows // blocks, width), lambda i: (i, 0)),
        scratch_shapes=[pltpu.VMEM((negs, width), BF16)],
    )


def solution(mesh):
    return jax.shard_map(
        per_device,
        mesh=mesh,
        in_specs=(
            P(("ent", "grp"), None),
            P(("ent", "grp"), None),
            P(("ent", "grp")),
            P(("ent", "grp")),
            P(("ent", "grp")),
            P(),
            P(),
            P(),
            P(),
            P(),
            P(),
        ),
        out_specs=P(("ent", "grp"), None),
        check_vma=False,
    )
```

```python
import functools
import math

import jax
import jax.numpy as jnp
from jax import lax
from jax.experimental import pallas as pl
from jax.experimental.pallas import tpu as pltpu
from jax.sharding import PartitionSpec as P

POS_WEIGHT = 64

norm_eps = 1e-06

F32 = jnp.float32
BF16 = jnp.bfloat16
I32 = jnp.int32

NN = (((1,), (0,)), ((), ()))
NT = (((1,), (1,)), ((), ()))
TN = (((0,), (0,)), ((), ()))


def dot(a, b, dims=NN):
    return lax.dot_general(a, b, dims, preferred_element_type=F32)


def in_hbm(*arrays):
    return tuple(pltpu.with_memory_space_constraint(array, pltpu.HBM) for array in arrays)


def iota(shape, axis):
    return lax.broadcasted_iota(I32, shape, axis)


def ones_where(mask):
    return jnp.where(mask, 1.0, 0.0).astype(BF16)


def to_column(row):
    count = row.shape[1]
    same = iota((count, count), 0) == iota((count, count), 1)
    return jnp.sum(jnp.where(same, row, 0.0), axis=1, keepdims=True)


def to_row(column):
    count = column.shape[0]
    same = iota((count, count), 0) == iota((count, count), 1)
    return jnp.sum(jnp.where(same, column, 0.0), axis=0, keepdims=True)


def split_bytes(numbers):
    high = jnp.floor(numbers * (1.0 / 256.0))
    return high.astype(BF16), (numbers - high * 256.0).astype(BF16)


def call(kernel, out_shape, args, flops, moved, **kwargs):
    return pl.pallas_call(
        kernel,
        out_shape=out_shape,
        compiler_params=pltpu.CompilerParams(vmem_limit_bytes=kwargs.pop("vmem", 28) << 20),
        cost_estimate=pl.CostEstimate(flops=flops, bytes_accessed=moved, transcendentals=0),
        **kwargs,
    )(*args)


def prepare_kernel(
    owner_ref,
    local_ref,
    neg_local_ref,
    table_ref,
    request_ref,
    slot_row_ref,
    neg_ref,
    small_ref,
    stage_ref,
    sem,
):
    parts, rows, _ = stage_ref.shape
    copies = [
        pltpu.make_async_copy(
            table_ref.at[pl.ds(part * rows, rows)], stage_ref.at[part], sem.at[part]
        )
        for part in range(parts)
    ]
    for copy in copies:
        copy.start()
    refs = owner_ref.shape[1]
    dev_count, capacity = request_ref.shape
    owner = to_column(owner_ref[...].astype(F32))
    hit = owner.astype(I32) == iota((refs, dev_count), 1)
    hit_one = ones_where(hit)
    earlier = ones_where(iota((refs, refs), 1) <= iota((refs, refs), 0))
    rank = dot(earlier, hit_one)
    placed = jnp.sum(jnp.where(hit, rank, 0.0), axis=1, keepdims=True) - 1.0
    slot = owner * float(capacity) + placed
    local = to_column(local_ref[...].astype(F32))
    at = placed.astype(I32) == iota((refs, capacity), 1)
    high, low = split_bytes(jnp.where(at, local, 0.0))
    request = dot(hit_one, high, TN) * 256.0 + dot(hit_one, low, TN)
    request_ref[...] = request.astype(I32)
    slot_row_ref[...] = to_row(slot).astype(I32)
    neg_local = to_column(neg_local_ref[...].astype(F32)).astype(I32)
    total = jnp.zeros(neg_ref.shape, F32)
    for part, copy in enumerate(copies):
        copy.wait()
        small = stage_ref[part].astype(BF16)
        small_ref[part * rows : (part + 1) * rows, :] = small
        hot = neg_local == iota((neg_ref.shape[0], rows), 1) + part * rows
        total = total + dot(ones_where(hot), small)
    neg_ref[...] = total.astype(BF16)


def fetch_kernel(pieces, *refs):
    wanted_ref, table_ref, out_ref = refs[pieces:]
    dev_count, capacity = wanted_ref.shape
    slots = out_ref.shape[0]
    rows = table_ref.shape[0]
    high, low = split_bytes(wanted_ref[...].astype(F32))
    first = iota((slots, dev_count), 1) * capacity
    slot = iota((slots, dev_count), 0)
    mine = ones_where((slot >= first) & (slot < first + capacity))
    spread = dot(mine, high) * 256.0 + dot(mine, low)
    at = lax.rem(iota((slots, capacity), 0), capacity) == iota((slots, capacity), 1)
    wanted = jnp.sum(jnp.where(at, spread, 0.0), axis=1, keepdims=True).astype(I32)
    block = math.gcd(slots, 256)
    for start in range(0, slots, block):
        hot = ones_where(wanted[start : start + block] == iota((block, rows), 1))
        out_ref[start : start + block, :] = dot(hot, table_ref[...]).astype(BF16)


def load_all(pairs, sem):
    copies = [
        pltpu.make_async_copy(source, buffer, sem.at[i])
        for i, (source, buffer) in enumerate(pairs)
    ]
    for copy in copies:
        copy.start()
    return copies


def encode_kernel(
    slot_ref,
    in_gain_ref,
    out_gain_ref,
    fetched_hbm,
    rel_hbm,
    gate_hbm,
    up_hbm,
    down_hbm,
    query_bf_ref,
    base_ref,
    ctx_ref,
    mixed_ref,
    silu_ref,
    slope_ref,
    fetched_ref,
    rel_ref,
    gate_ref,
    up_ref,
    down_ref,
    sem,
):
    loads = load_all(
        (
            (fetched_hbm, fetched_ref),
            (rel_hbm, rel_ref),
            (gate_hbm, gate_ref),
            (up_hbm, up_ref),
            (down_hbm, down_ref),
        ),
        sem,
    )
    queries = rel_ref.shape[0]
    refs = slot_ref.shape[1]
    slots = fetched_ref.shape[0]
    slot = to_column(slot_ref[...].astype(F32)).astype(I32)
    pick = ones_where(slot == iota((refs, slots), 1))
    loads[0].wait()
    head = dot(pick[:queries], fetched_ref[...])
    loads[1].wait()
    base = head + rel_ref[...]
    base_ref[...] = base
    in_scale = lax.rsqrt(jnp.mean(base * base, axis=-1, keepdims=True) + norm_eps)
    normed = (base * in_scale * in_gain_ref[...]).astype(BF16)
    ctx_ref[...] = dot(pick[queries:], fetched_ref[...]).astype(BF16)
    loads[2].wait()
    gate = dot(normed, gate_ref[...])
    loads[3].wait()
    up = dot(normed, up_ref[...])
    sig = jax.nn.sigmoid(gate)
    silu = gate * sig
    hidden = (silu * up).astype(BF16)
    silu_ref[...] = silu.astype(BF16)
    slope_ref[...] = (up * (sig + silu * (1.0 - sig))).astype(BF16)
    loads[4].wait()
    mixed = base + dot(hidden, down_ref[...])
    mixed_ref[...] = mixed
    out_scale = lax.rsqrt(jnp.mean(mixed * mixed, axis=-1, keepdims=True) + norm_eps)
    query_bf_ref[...] = (mixed * out_scale * out_gain_ref[...]).astype(BF16)


def norm_pull(value, gain, cotangent):
    scale = lax.rsqrt(jnp.mean(value * value, axis=-1, keepdims=True) + norm_eps)
    scaled = cotangent * gain
    along = jnp.mean(scaled * value, axis=-1, keepdims=True)
    return scale * scaled - value * (along * scale * scale * scale)


def grad_kernel(inv_scale, pieces, *refs):
    slot_ref, in_gain_ref, out_gain_ref, query_ref, mixed_ref, ctx_ref = refs[:6]
    silu_ref, slope_ref, base_ref = refs[6:9]
    neg_refs = refs[9 : pieces + 9]
    sources = refs[pieces + 9 : pieces + 12]
    out_ref, down_ref, gate_ref, up_ref, sem = refs[pieces + 12 :]
    loads = load_all(zip(sources, (down_ref, gate_ref, up_ref)), sem)
    mixed = mixed_ref[...]
    out_scale = lax.rsqrt(jnp.mean(mixed * mixed, axis=-1, keepdims=True) + norm_eps)
    query = mixed * out_scale * out_gain_ref[...]
    query_bf = query_ref[...]
    ctx = ctx_ref[...].astype(F32)
    pos_score = jnp.sum(query * ctx, axis=-1, keepdims=True) * inv_scale
    pos_weight = POS_WEIGHT * (jax.nn.sigmoid(pos_score) - 1.0) * inv_scale
    query_grad = pos_weight * ctx
    for neg_ref in neg_refs:
        neg = neg_ref[...]
        scores = dot(query_bf, neg, NT) * inv_scale
        weight = (jax.nn.sigmoid(scores) * inv_scale).astype(BF16)
        query_grad = query_grad + dot(weight, neg)
    ctx_grad = (pos_weight * query).astype(BF16)
    mixed_cot = norm_pull(mixed, out_gain_ref[...], query_grad)
    loads[0].wait()
    hidden_cot = dot(mixed_cot.astype(BF16), down_ref[...], NT).astype(BF16).astype(F32)
    up_cot = (hidden_cot * silu_ref[...].astype(F32)).astype(BF16)
    gate_cot = (hidden_cot * slope_ref[...].astype(F32)).astype(BF16)
    loads[1].wait()
    normed_cot = dot(gate_cot, gate_ref[...], NT)
    loads[2].wait()
    normed_cot = normed_cot + dot(up_cot, up_ref[...], NT)
    normed_cot = normed_cot.astype(BF16).astype(F32)
    head_grad = mixed_cot + norm_pull(base_ref[...], in_gain_ref[...], normed_cot)
    slots = out_ref.shape[0]
    queries = query.shape[0]
    slot = slot_ref[...]
    place = ones_where(iota((slots, slot.shape[1]), 0) == slot)
    out = dot(place[:, :queries], head_grad.astype(BF16)) + dot(place[:, queries:], ctx_grad)
    out_ref[...] = out.astype(BF16)


def neg_grad_kernel(inv_scale, pieces, *refs):
    query_refs = refs[:pieces]
    neg_ref, out_ref = refs[pieces:]
    neg = neg_ref[...]
    total = jnp.zeros(neg.shape, F32)
    for query_ref in query_refs:
        query = query_ref[...]
        scores = dot(neg, query, NT) * inv_scale
        weight = (jax.nn.sigmoid(scores) * inv_scale).astype(BF16)
        total = total + dot(weight, query)
    out_ref[...] = total.astype(out_ref.dtype)


def wanted_row_kernel(wanted_ref, out_ref):
    dev_count, capacity = wanted_ref.shape
    slots = out_ref.shape[1]
    high, low = split_bytes(wanted_ref[...].astype(F32))
    at = ones_where(
        lax.rem(iota((capacity, slots), 1), capacity) == iota((capacity, slots), 0)
    )
    spread = dot(high, at) * 256.0 + dot(low, at)
    first = iota((dev_count, slots), 0) * capacity
    slot = iota((dev_count, slots), 1)
    mine = (slot >= first) & (slot < first + capacity)
    out_ref[...] = jnp.sum(jnp.where(mine, spread, 0.0), axis=0, keepdims=True).astype(I32)


def scatter_kernel(parts, *refs):
    sent_refs = refs[:parts]
    wanted_ref, local_ref, back_ref, own_ref, out_ref, neg_ref = refs[parts:]
    slots = back_ref.shape[0]
    rows = out_ref.shape[0]

    @pl.when(pl.program_id(0) == 0)
    def _():
        total = own_ref[...]
        for sent_ref in sent_refs:
            total = total + sent_ref[...].astype(F32)
        neg_ref[...] = total.astype(BF16)

    start = pl.program_id(0) * rows
    place = ones_where(iota((rows, slots), 0) + start == wanted_ref[...])
    local = local_ref[...]
    spot = ones_where(iota((rows, local.shape[1]), 0) + start == local)
    out_ref[...] = dot(place, back_ref[...]) + dot(spot, neg_ref[...])


def grid_inner(count):
    return 1 << ((count.bit_length() - 1) // 2)


def flip(block, axis, step):
    count = lax.axis_size(axis)
    return lax.ppermute(block, axis, [(i, i ^ step) for i in range(count)])


def spread_over(block, axis, others):
    held = {0: block}
    for other in sorted(others, key=lambda n: (bin(n).count("1"), -n)):
        step = other & -other
        held[other] = flip(held[other - step], axis, step)
    return held


def per_device(
    table,
    touch_owner,
    touch_local,
    query_rel,
    neg_local,
    rel_table,
    in_gain,
    out_gain,
    w_gate,
    w_up,
    w_down,
):
    axes = ("ent", "grp")
    dev_count = lax.axis_size("ent") * lax.axis_size("grp")
    refs = touch_local.shape[0]
    queries = refs // 2
    capacity = 2 * refs // dev_count
    slots = dev_count * capacity
    rows, width = table.shape
    hidden = w_gate.shape[1]
    negs = neg_local.shape[0]
    inv_scale = 1.0 / math.sqrt(width)
    shape = jax.ShapeDtypeStruct
    in_gain = in_gain.reshape(1, width)
    out_gain = out_gain.reshape(1, width)
    neg_row = neg_local.reshape(1, negs)

    group = lax.axis_size("grp")
    inner = grid_inner(group)
    hbm = pl.BlockSpec(memory_space=pl.ANY)
    vmem = pl.BlockSpec(memory_space=pltpu.VMEM)

    parts = 4 if rows % 64 == 0 else 1
    requests, slot_row, neg_rows, small_table = call(
        prepare_kernel,
        (
            shape((dev_count, capacity), I32),
            shape((1, refs), I32),
            shape((negs, width), BF16),
            shape((rows, width), BF16),
        ),
        in_hbm(touch_owner.reshape(1, refs), touch_local.reshape(1, refs), neg_row, table),
        2 * negs * rows * width,
        6 * rows * width,
        in_specs=[vmem, vmem, vmem, hbm],
        scratch_shapes=[
            pltpu.VMEM((parts, rows // parts, width), F32),
            pltpu.SemaphoreType.DMA((parts,)),
        ],
    )
    neg_held = spread_over(neg_rows, "grp", range(1, group))
    neg_pieces = [neg_held[other] for other in range(group)]
    wanted = lax.all_to_all(requests, axes, split_axis=0, concat_axis=0, tiled=True)

    ahead = [neg_held[1 << bit] for bit in range(group.bit_length() - 1)]
    looked = call(
        functools.partial(fetch_kernel, len(ahead)),
        pltpu.HBM((slots, width), BF16),
        (*ahead, wanted, small_table),
        2 * slots * rows * width,
        2 * (slots + rows) * width,
        in_specs=[pl.BlockSpec(memory_space=pl.ANY)] * len(ahead) + [vmem, vmem],
    )
    fetched = lax.all_to_all(
        looked.reshape(dev_count, capacity, width), axes, split_axis=0, concat_axis=0, tiled=True
    ).reshape(slots, width)

    rel_onehot = (
        query_rel[:, None] == jnp.arange(rel_table.shape[0], dtype=jnp.int32)[None, :]
    ).astype(BF16)
    rel_rows = jnp.dot(rel_onehot, rel_table, preferred_element_type=F32)

    def buffer(array):
        return pltpu.VMEM(array.shape, array.dtype)

    sources = (fetched, rel_rows, w_gate, w_up, w_down)
    outputs = (
        shape((queries, width), BF16),
        shape((queries, width), F32),
        shape((queries, width), BF16),
        shape((queries, width), F32),
        shape((queries, hidden), BF16),
        shape((queries, hidden), BF16),
    )
    query_bf, base, ctx, mixed, silu, slope = call(
        encode_kernel,
        outputs,
        in_hbm(slot_row, in_gain, out_gain, *sources),
        2 * queries * width * (2 * slots + 3 * hidden),
        2 * (slots * width + 3 * width * hidden),
        in_specs=[vmem] * 3 + [hbm] * 5,
        scratch_shapes=[buffer(a) for a in sources] + [pltpu.SemaphoreType.DMA((5,))],
    )
    query_held = spread_over(query_bf, "grp", range(inner, group, inner))
    query_pieces = list(query_held.values())

    weights = (w_down, w_gate, w_up)
    outgoing = call(
        functools.partial(grad_kernel, inv_scale, len(neg_pieces)),
        pltpu.HBM((slots, width), BF16),
        in_hbm(slot_row, in_gain, out_gain)
        + (query_bf, mixed, ctx, silu, slope, base, *neg_pieces)
        + in_hbm(*weights),
        2 * queries * width * (2 * slots + 3 * hidden + 2 * negs * len(neg_pieces)),
        2 * (slots * width + 3 * width * hidden + negs * width * len(neg_pieces)),
        in_specs=[vmem] * (len(neg_pieces) + 9) + [hbm] * 3,
        scratch_shapes=[buffer(a) for a in weights] + [pltpu.SemaphoreType.DMA((3,))],
    )
    early = [query_held[step] for step in query_held if step and step & (step - 1) == 0]
    outgoing, *_ = lax.optimization_barrier((outgoing, *early))
    returned = lax.all_to_all(
        outgoing.reshape(dev_count, capacity, width), axes, split_axis=0, concat_axis=0, tiled=True
    ).reshape(slots, width)

    def neg_grad(other, dtype):
        return call(
            functools.partial(neg_grad_kernel, inv_scale, len(query_pieces)),
            pltpu.HBM((negs, width), dtype) if other == 0 else shape((negs, width), dtype),
            (*query_pieces, neg_held[other]),
            4 * queries * negs * width * len(query_pieces),
            2 * queries * width * len(query_pieces),
        )

    sent = [flip(neg_grad(other, BF16), "grp", other) for other in range(1, inner)]
    own = neg_grad(0, F32)
    wanted_row = call(
        wanted_row_kernel, pltpu.HBM((1, slots), I32), (wanted,), slots * dev_count, 4 * slots
    )

    blocks = 4 if rows % 64 == 0 else 1
    whole = lambda a: pl.BlockSpec(a.shape, lambda i: (0, 0))
    operands = in_hbm(*sent, wanted_row, neg_row) + (returned,) + in_hbm(own)
    return call(
        functools.partial(scatter_kernel, len(sent)),
        shape((rows, width), F32),
        operands,
        2 * rows * width * (slots + negs),
        4 * rows * width + 2 * slots * width,
        grid=(blocks,),
        in_specs=[whole(a) for a in operands],
        out_specs=pl.BlockSpec((rows // blocks, width), lambda i: (i, 0)),
        scratch_shapes=[pltpu.VMEM((negs, width), BF16)],
    )


def solution(mesh):
    return jax.shard_map(
        per_device,
        mesh=mesh,
        in_specs=(
            P(("ent", "grp"), None),
            P(("ent", "grp"), None),
            P(("ent", "grp")),
            P(("ent", "grp")),
            P(("ent", "grp")),
            P(),
            P(),
            P(),
            P(),
            P(),
            P(),
        ),
        out_specs=P(("ent", "grp"), None),
        check_vma=False,
    )
```

```python
import functools
import math

import jax
import jax.numpy as jnp
from jax import lax
from jax.experimental import pallas as pl
from jax.experimental.pallas import tpu as pltpu
from jax.sharding import PartitionSpec as P

POS_WEIGHT = 64

norm_eps = 1e-06

SHADOW_FLOPS = 1 << 45

F32 = jnp.float32
BF16 = jnp.bfloat16
I32 = jnp.int32

NN = (((1,), (0,)), ((), ()))
NT = (((1,), (1,)), ((), ()))
TN = (((0,), (0,)), ((), ()))


def dot(a, b, dims=NN):
    return lax.dot_general(a, b, dims, preferred_element_type=F32)


def in_hbm(*arrays):
    return tuple(pltpu.with_memory_space_constraint(array, pltpu.HBM) for array in arrays)


def iota(shape, axis):
    return lax.broadcasted_iota(I32, shape, axis)


def ones_where(mask):
    return jnp.where(mask, 1.0, 0.0).astype(BF16)


def to_column(row):
    count = row.shape[1]
    same = iota((count, count), 0) == iota((count, count), 1)
    return jnp.sum(jnp.where(same, row, 0.0), axis=1, keepdims=True)


def to_row(column):
    count = column.shape[0]
    same = iota((count, count), 0) == iota((count, count), 1)
    return jnp.sum(jnp.where(same, column, 0.0), axis=0, keepdims=True)


def split_bytes(numbers):
    high = jnp.floor(numbers * (1.0 / 256.0))
    return high.astype(BF16), (numbers - high * 256.0).astype(BF16)


def call(kernel, out_shape, args, flops, moved, **kwargs):
    return pl.pallas_call(
        kernel,
        out_shape=out_shape,
        compiler_params=pltpu.CompilerParams(vmem_limit_bytes=kwargs.pop("vmem", 28) << 20),
        cost_estimate=pl.CostEstimate(flops=flops, bytes_accessed=moved, transcendentals=0),
        **kwargs,
    )(*args)


def prepare_kernel(
    owner_ref,
    local_ref,
    neg_local_ref,
    table_ref,
    request_ref,
    slot_row_ref,
    neg_ref,
    small_ref,
    stage_ref,
    sem,
):
    parts, rows, _ = stage_ref.shape
    copies = [
        pltpu.make_async_copy(
            table_ref.at[pl.ds(part * rows, rows)], stage_ref.at[part], sem.at[part]
        )
        for part in range(parts)
    ]
    for copy in copies:
        copy.start()
    refs = owner_ref.shape[1]
    dev_count, capacity = request_ref.shape
    owner = to_column(owner_ref[...].astype(F32))
    hit = owner.astype(I32) == iota((refs, dev_count), 1)
    hit_one = ones_where(hit)
    earlier = ones_where(iota((refs, refs), 1) <= iota((refs, refs), 0))
    rank = dot(earlier, hit_one)
    placed = jnp.sum(jnp.where(hit, rank, 0.0), axis=1, keepdims=True) - 1.0
    slot = owner * float(capacity) + placed
    local = to_column(local_ref[...].astype(F32))
    at = placed.astype(I32) == iota((refs, capacity), 1)
    high, low = split_bytes(jnp.where(at, local, 0.0))
    request = dot(hit_one, high, TN) * 256.0 + dot(hit_one, low, TN)
    request_ref[...] = request.astype(I32)
    slot_row_ref[...] = to_row(slot).astype(I32)
    neg_local = to_column(neg_local_ref[...].astype(F32)).astype(I32)
    total = jnp.zeros(neg_ref.shape, F32)
    for part, copy in enumerate(copies):
        copy.wait()
        small = stage_ref[part].astype(BF16)
        small_ref[part * rows : (part + 1) * rows, :] = small
        hot = neg_local == iota((neg_ref.shape[0], rows), 1) + part * rows
        total = total + dot(ones_where(hot), small)
    neg_ref[...] = total.astype(BF16)


def fetch_kernel(pieces, *refs):
    wanted_ref, table_ref, out_ref, stage_ref, sem = refs[pieces:]
    dev_count, capacity = wanted_ref.shape
    slots = out_ref.shape[0]
    rows = table_ref.shape[0]
    high, low = split_bytes(wanted_ref[...].astype(F32))
    first = iota((slots, dev_count), 1) * capacity
    slot = iota((slots, dev_count), 0)
    mine = ones_where((slot >= first) & (slot < first + capacity))
    spread = dot(mine, high) * 256.0 + dot(mine, low)
    at = lax.rem(iota((slots, capacity), 0), capacity) == iota((slots, capacity), 1)
    wanted = jnp.sum(jnp.where(at, spread, 0.0), axis=1, keepdims=True).astype(I32)
    block = stage_ref.shape[1]
    stores = []
    for part in range(stage_ref.shape[0]):
        start = part * block
        hot = ones_where(wanted[start : start + block] == iota((block, rows), 1))
        stage_ref[part] = dot(hot, table_ref[...]).astype(BF16)
        store = pltpu.make_async_copy(
            stage_ref.at[part], out_ref.at[pl.ds(start, block)], sem.at[part]
        )
        store.start()
        stores.append(store)
    for store in stores:
        store.wait()


def relation_kernel(rel_ref, table_ref, out_ref):
    rel = to_column(rel_ref[...].astype(F32)).astype(I32)
    hot = ones_where(rel == iota((rel.shape[0], table_ref.shape[0]), 1))
    out_ref[...] = dot(hot, table_ref[...]).astype(BF16)


def load_all(pairs, sem):
    copies = [
        pltpu.make_async_copy(source, buffer, sem.at[i])
        for i, (source, buffer) in enumerate(pairs)
    ]
    for copy in copies:
        copy.start()
    return copies


def encode_kernel(
    slot_ref,
    in_gain_ref,
    out_gain_ref,
    fetched_hbm,
    rel_hbm,
    gate_hbm,
    up_hbm,
    down_hbm,
    query_bf_ref,
    base_ref,
    ctx_ref,
    mixed_ref,
    silu_ref,
    slope_ref,
    fetched_ref,
    rel_ref,
    gate_ref,
    up_ref,
    down_ref,
    sem,
):
    loads = load_all(
        (
            (fetched_hbm, fetched_ref),
            (rel_hbm, rel_ref),
            (gate_hbm, gate_ref),
            (up_hbm, up_ref),
            (down_hbm, down_ref),
        ),
        sem,
    )
    queries = rel_ref.shape[0]
    refs = slot_ref.shape[1]
    slots = fetched_ref.shape[0]
    slot = to_column(slot_ref[...].astype(F32)).astype(I32)
    pick = ones_where(slot == iota((refs, slots), 1))
    loads[0].wait()
    head = dot(pick[:queries], fetched_ref[...])
    loads[1].wait()
    base = head + rel_ref[...].astype(F32)
    base_ref[...] = base
    in_scale = lax.rsqrt(jnp.mean(base * base, axis=-1, keepdims=True) + norm_eps)
    normed = (base * in_scale * in_gain_ref[...]).astype(BF16)
    ctx_ref[...] = dot(pick[queries:], fetched_ref[...]).astype(BF16)
    loads[2].wait()
    gate = dot(normed, gate_ref[...])
    loads[3].wait()
    up = dot(normed, up_ref[...])
    sig = jax.nn.sigmoid(gate)
    silu = gate * sig
    hidden = (silu * up).astype(BF16)
    silu_ref[...] = silu.astype(BF16)
    slope_ref[...] = (up * (sig + silu * (1.0 - sig))).astype(BF16)
    loads[4].wait()
    mixed = base + dot(hidden, down_ref[...])
    mixed_ref[...] = mixed
    out_scale = lax.rsqrt(jnp.mean(mixed * mixed, axis=-1, keepdims=True) + norm_eps)
    query_bf_ref[...] = (mixed * out_scale * out_gain_ref[...]).astype(BF16)


def norm_pull(value, gain, cotangent):
    scale = lax.rsqrt(jnp.mean(value * value, axis=-1, keepdims=True) + norm_eps)
    scaled = cotangent * gain
    along = jnp.mean(scaled * value, axis=-1, keepdims=True)
    return scale * scaled - value * (along * scale * scale * scale)


def grad_kernel(inv_scale, pieces, *refs):
    slot_ref, in_gain_ref, out_gain_ref, query_ref, mixed_ref, ctx_ref = refs[:6]
    silu_ref, slope_ref, base_ref = refs[6:9]
    neg_refs = refs[9 : pieces + 9]
    sources = refs[pieces + 9 : pieces + 12]
    out_ref, down_ref, gate_ref, up_ref, stage_ref, sem, out_sem = refs[pieces + 12 :]
    loads = load_all(zip(sources, (down_ref, gate_ref, up_ref)), sem)
    mixed = mixed_ref[...]
    out_scale = lax.rsqrt(jnp.mean(mixed * mixed, axis=-1, keepdims=True) + norm_eps)
    query = mixed * out_scale * out_gain_ref[...]
    query_bf = query_ref[...]
    ctx = ctx_ref[...].astype(F32)
    pos_score = jnp.sum(query * ctx, axis=-1, keepdims=True) * inv_scale
    pos_weight = POS_WEIGHT * (jax.nn.sigmoid(pos_score) - 1.0) * inv_scale
    query_grad = pos_weight * ctx
    for neg_ref in neg_refs:
        neg = neg_ref[...]
        scores = dot(query_bf, neg, NT) * inv_scale
        weight = (jax.nn.sigmoid(scores) * inv_scale).astype(BF16)
        query_grad = query_grad + dot(weight, neg)
    ctx_grad = (pos_weight * query).astype(BF16)
    mixed_cot = norm_pull(mixed, out_gain_ref[...], query_grad)
    loads[0].wait()
    hidden_cot = dot(mixed_cot.astype(BF16), down_ref[...], NT).astype(BF16).astype(F32)
    up_cot = (hidden_cot * silu_ref[...].astype(F32)).astype(BF16)
    gate_cot = (hidden_cot * slope_ref[...].astype(F32)).astype(BF16)
    loads[1].wait()
    normed_cot = dot(gate_cot, gate_ref[...], NT)
    loads[2].wait()
    normed_cot = normed_cot + dot(up_cot, up_ref[...], NT)
    normed_cot = normed_cot.astype(BF16).astype(F32)
    head_grad = mixed_cot + norm_pull(base_ref[...], in_gain_ref[...], normed_cot)
    head_grad = head_grad.astype(BF16)
    queries = query.shape[0]
    slot = slot_ref[...]
    block = stage_ref.shape[1]
    stores = []
    for part in range(stage_ref.shape[0]):
        start = part * block
        place = ones_where(iota((block, slot.shape[1]), 0) + start == slot)
        out = dot(place[:, :queries], head_grad) + dot(place[:, queries:], ctx_grad)
        stage_ref[part] = out.astype(BF16)
        store = pltpu.make_async_copy(
            stage_ref.at[part], out_ref.at[pl.ds(start, block)], out_sem.at[part]
        )
        store.start()
        stores.append(store)
    for store in stores:
        store.wait()


def neg_grad_kernel(inv_scale, pieces, blocks, *refs):
    query_refs, neg_refs = refs[:pieces], refs[pieces : pieces + blocks]
    before_refs, out_refs = refs[pieces + blocks : -blocks], refs[-blocks:]
    for i in reversed(range(blocks)):
        neg = neg_refs[i][...]
        total = before_refs[i][...] if before_refs else jnp.zeros(neg.shape, F32)
        for query_ref in query_refs:
            query = query_ref[...]
            scores = dot(neg, query, NT) * inv_scale
            weight = (jax.nn.sigmoid(scores) * inv_scale).astype(BF16)
            total = total + dot(weight, query)
        out_refs[i][...] = total.astype(out_refs[i].dtype)


def wanted_row_kernel(wanted_ref, out_ref):
    dev_count, capacity = wanted_ref.shape
    slots = out_ref.shape[1]
    high, low = split_bytes(wanted_ref[...].astype(F32))
    at = ones_where(
        lax.rem(iota((capacity, slots), 1), capacity) == iota((capacity, slots), 0)
    )
    spread = dot(high, at) * 256.0 + dot(low, at)
    first = iota((dev_count, slots), 0) * capacity
    slot = iota((dev_count, slots), 1)
    mine = (slot >= first) & (slot < first + capacity)
    out_ref[...] = jnp.sum(jnp.where(mine, spread, 0.0), axis=0, keepdims=True).astype(I32)


def scatter_kernel(parts, *refs):
    sent_refs = refs[:parts]
    wanted_ref, local_ref, back_ref, own_ref, out_ref, stage_ref, sem = refs[parts:]
    slots = back_ref.shape[0]
    neg = own_ref[...]
    for sent_ref in sent_refs:
        neg = neg + sent_ref[...].astype(F32)
    neg = neg.astype(BF16)
    wanted = wanted_ref[...]
    local = local_ref[...]
    blocks, rows, _ = stage_ref.shape
    stores = []
    for block in range(blocks):
        start = block * rows
        place = ones_where(iota((rows, slots), 0) + start == wanted)
        spot = ones_where(iota((rows, local.shape[1]), 0) + start == local)
        stage_ref[block] = dot(place, back_ref[...]) + dot(spot, neg)
        store = pltpu.make_async_copy(
            stage_ref.at[block], out_ref.at[pl.ds(start, rows)], sem.at[block]
        )
        store.start()
        stores.append(store)
    for store in stores:
        store.wait()


def flip(block, axis, step):
    count = lax.axis_size(axis)
    return lax.ppermute(block, axis, [(i, i ^ step) for i in range(count)])


def spread_over(block, axis, others, beside):
    held = {0: block}
    for other in sorted(others, key=lambda n: (bin(n).count("1"), -n)):
        step = other & -other
        source = held[other - step]
        if other == 3:
            source, _ = lax.optimization_barrier((source, beside))
        held[other] = flip(source, axis, step)
    return held


def per_device(
    table,
    touch_owner,
    touch_local,
    query_rel,
    neg_local,
    rel_table,
    in_gain,
    out_gain,
    w_gate,
    w_up,
    w_down,
):
    axes = ("ent", "grp")
    dev_count = lax.axis_size("ent") * lax.axis_size("grp")
    refs = touch_local.shape[0]
    queries = refs // 2
    capacity = 2 * refs // dev_count
    slots = dev_count * capacity
    rows, width = table.shape
    hidden = w_gate.shape[1]
    negs = neg_local.shape[0]
    inv_scale = 1.0 / math.sqrt(width)
    shape = jax.ShapeDtypeStruct
    in_gain = in_gain.reshape(1, width)
    out_gain = out_gain.reshape(1, width)
    neg_row = neg_local.reshape(1, negs)

    group = lax.axis_size("grp")
    half = group // 2
    hbm = pl.BlockSpec(memory_space=pl.ANY)
    vmem = pl.BlockSpec(memory_space=pltpu.VMEM)

    parts = 4 if rows % 64 == 0 else 1
    requests, slot_row, neg_rows, small_table = call(
        prepare_kernel,
        (
            shape((dev_count, capacity), I32),
            shape((1, refs), I32),
            shape((negs, width), BF16),
            shape((rows, width), BF16),
        ),
        in_hbm(touch_owner.reshape(1, refs), touch_local.reshape(1, refs), neg_row, table),
        2 * negs * rows * width,
        6 * rows * width,
        in_specs=[vmem, vmem, vmem, hbm],
        scratch_shapes=[
            pltpu.VMEM((parts, rows // parts, width), F32),
            pltpu.SemaphoreType.DMA((parts,)),
        ],
    )
    rel_rows = call(
        relation_kernel,
        pltpu.HBM((queries, width), BF16),
        in_hbm(query_rel.reshape(1, queries), rel_table),
        2 * queries * rel_table.size,
        2 * rel_table.size,
    )

    neg_held = spread_over(neg_rows, "grp", range(1, group), rel_rows)
    neg_pieces = [neg_held[other] for other in range(group)]
    wanted = lax.all_to_all(requests, axes, split_axis=0, concat_axis=0, tiled=True)

    ahead = [neg_held[1 << bit] for bit in range(group.bit_length() - 1)]
    block = math.gcd(slots, 256)
    looked = call(
        functools.partial(fetch_kernel, len(ahead)),
        pltpu.HBM((slots, width), BF16),
        (*ahead, wanted, small_table),
        2 * slots * rows * width,
        2 * (slots + rows) * width,
        in_specs=[hbm] * len(ahead) + [vmem, vmem],
        out_specs=hbm,
        scratch_shapes=[
            pltpu.VMEM((slots // block, block, width), BF16),
            pltpu.SemaphoreType.DMA((slots // block,)),
        ],
    )
    fetched = lax.all_to_all(
        looked.reshape(dev_count, capacity, width), axes, split_axis=0, concat_axis=0, tiled=True
    ).reshape(slots, width)

    def buffer(array):
        return pltpu.VMEM(array.shape, array.dtype)

    sources = (fetched, rel_rows, w_gate, w_up, w_down)
    outputs = (
        shape((queries, width), BF16),
        shape((queries, width), F32),
        shape((queries, width), BF16),
        shape((queries, width), F32),
        shape((queries, hidden), BF16),
        shape((queries, hidden), BF16),
    )
    query_bf, base, ctx, mixed, silu, slope = call(
        encode_kernel,
        outputs,
        in_hbm(slot_row, in_gain, out_gain) + (fetched,) + in_hbm(*sources[1:]),
        2 * queries * width * (2 * slots + 3 * hidden),
        2 * (slots * width + 3 * width * hidden),
        in_specs=[vmem] * 3 + [hbm] * 5,
        scratch_shapes=[buffer(a) for a in sources] + [pltpu.SemaphoreType.DMA((5,))],
    )
    low = 1 if group > 2 else 0
    near = [query_bf, flip(query_bf, "grp", half)] + ([flip(query_bf, "grp", low)] if low else [])
    far = [flip(near[1], "grp", low)] if low else []
    others = [other for other in range(1, group) if not other & (low | half)]

    weights = (w_down, w_gate, w_up)
    outgoing = call(
        functools.partial(grad_kernel, inv_scale, len(neg_pieces)),
        pltpu.HBM((slots, width), BF16),
        in_hbm(slot_row, in_gain, out_gain)
        + (query_bf, mixed, ctx, silu, slope, base, *neg_pieces)
        + in_hbm(*weights),
        2 * queries * width * (2 * slots + 3 * hidden + 2 * negs * len(neg_pieces)),
        2 * (slots * width + 3 * width * hidden + negs * width * len(neg_pieces)),
        in_specs=[vmem] * (len(neg_pieces) + 9) + [hbm] * 3,
        out_specs=hbm,
        scratch_shapes=[buffer(a) for a in weights]
        + [
            pltpu.VMEM((slots // block, block, width), BF16),
            pltpu.SemaphoreType.DMA((3,)),
            pltpu.SemaphoreType.DMA((slots // block,)),
        ],
    )
    returned = lax.all_to_all(
        outgoing.reshape(dev_count, capacity, width), axes, split_axis=0, concat_axis=0, tiled=True
    ).reshape(slots, width)

    blocks = 1 + len(others)
    neg_blocks = [neg_held[other] for other in [0] + others]
    first = call(
        functools.partial(neg_grad_kernel, inv_scale, len(near), blocks),
        [shape((negs, width), F32)] * blocks,
        (*near, *neg_blocks),
        SHADOW_FLOPS,
        2 * (len(near) + blocks) * negs * width,
    )
    def add_far(i, out):
        return call(
            functools.partial(neg_grad_kernel, inv_scale, len(far), 1),
            (out,),
            (*far, neg_blocks[i], first[i]),
            4 * len(far) * queries * negs * width,
            2 * (len(far) + 1) * negs * width,
        )[0]

    sums = [add_far(i, shape((negs, width), BF16)) for i in range(1, blocks)]
    own = add_far(0, pltpu.HBM((negs, width), F32))
    sent = [flip(block, "grp", other) for other, block in zip(others, sums)]
    wanted_row = call(
        wanted_row_kernel, pltpu.HBM((1, slots), I32), (wanted,), slots * dev_count, 4 * slots
    )

    parts = 8 if rows % 128 == 0 else 1
    return call(
        functools.partial(scatter_kernel, len(sent)),
        shape((rows, width), F32),
        (*sent, *in_hbm(wanted_row, neg_row), returned, *in_hbm(own)),
        2 * rows * width * (slots + negs),
        4 * rows * width + 2 * slots * width,
        out_specs=hbm,
        scratch_shapes=[
            pltpu.VMEM((parts, rows // parts, width), F32),
            pltpu.SemaphoreType.DMA((parts,)),
        ],
    )


def solution(mesh):
    return jax.shard_map(
        per_device,
        mesh=mesh,
        in_specs=(
            P(("ent", "grp"), None),
            P(("ent", "grp"), None),
            P(("ent", "grp")),
            P(("ent", "grp")),
            P(("ent", "grp")),
            P(),
            P(),
            P(),
            P(),
            P(),
            P(),
        ),
        out_specs=P(("ent", "grp"), None),
        check_vma=False,
    )
```

```python
import functools
import math

import jax
import jax.numpy as jnp
from jax import lax
from jax.experimental import pallas as pl
from jax.experimental.pallas import tpu as pltpu
from jax.sharding import PartitionSpec as P

POS_WEIGHT = 64

norm_eps = 1e-06

SHADOW_FLOPS = 1 << 45

F32 = jnp.float32
BF16 = jnp.bfloat16
I32 = jnp.int32

NN = (((1,), (0,)), ((), ()))
NT = (((1,), (1,)), ((), ()))
TN = (((0,), (0,)), ((), ()))


def dot(a, b, dims=NN):
    return lax.dot_general(a, b, dims, preferred_element_type=F32)


def in_hbm(*arrays):
    return tuple(pltpu.with_memory_space_constraint(array, pltpu.HBM) for array in arrays)


def iota(shape, axis):
    return lax.broadcasted_iota(I32, shape, axis)


def ones_where(mask):
    return jnp.where(mask, 1.0, 0.0).astype(BF16)


def to_column(row):
    count = row.shape[1]
    same = iota((count, count), 0) == iota((count, count), 1)
    return jnp.sum(jnp.where(same, row, 0.0), axis=1, keepdims=True)


def to_row(column):
    count = column.shape[0]
    same = iota((count, count), 0) == iota((count, count), 1)
    return jnp.sum(jnp.where(same, column, 0.0), axis=0, keepdims=True)


def split_bytes(numbers):
    high = jnp.floor(numbers * (1.0 / 256.0))
    return high.astype(BF16), (numbers - high * 256.0).astype(BF16)


def call(kernel, out_shape, args, flops, moved, **kwargs):
    return pl.pallas_call(
        kernel,
        out_shape=out_shape,
        compiler_params=pltpu.CompilerParams(vmem_limit_bytes=kwargs.pop("vmem", 28) << 20),
        cost_estimate=pl.CostEstimate(flops=flops, bytes_accessed=moved, transcendentals=0),
        **kwargs,
    )(*args)


def route_kernel(owner_ref, local_ref, request_ref, slot_row_ref):
    refs = owner_ref.shape[1]
    dev_count, capacity = request_ref.shape
    owner = to_column(owner_ref[...].astype(F32))
    hit = owner.astype(I32) == iota((refs, dev_count), 1)
    hit_one = ones_where(hit)
    earlier = ones_where(iota((refs, refs), 1) <= iota((refs, refs), 0))
    rank = dot(earlier, hit_one)
    placed = jnp.sum(jnp.where(hit, rank, 0.0), axis=1, keepdims=True) - 1.0
    slot = owner * float(capacity) + placed
    local = to_column(local_ref[...].astype(F32))
    at = placed.astype(I32) == iota((refs, capacity), 1)
    high, low = split_bytes(jnp.where(at, local, 0.0))
    request = dot(hit_one, high, TN) * 256.0 + dot(hit_one, low, TN)
    request_ref[...] = request.astype(I32)
    slot_row_ref[...] = to_row(slot).astype(I32)


def negatives_kernel(neg_local_ref, table_ref, neg_ref, small_ref, stage_ref, sem):
    parts, rows, _ = stage_ref.shape
    copies = load_all(
        [
            (table_ref.at[pl.ds(part * rows, rows)], stage_ref.at[part])
            for part in range(parts)
        ],
        sem,
    )
    neg_local = to_column(neg_local_ref[...].astype(F32)).astype(I32)
    total = jnp.zeros(neg_ref.shape, F32)
    for part, copy in enumerate(copies):
        copy.wait()
        small = stage_ref[part].astype(BF16)
        small_ref[part * rows : (part + 1) * rows, :] = small
        hot = neg_local == iota((neg_ref.shape[0], rows), 1) + part * rows
        total = total + dot(ones_where(hot), small)
    neg_ref[...] = total.astype(BF16)


def fetch_kernel(wanted_ref, table_ref, out_ref, stage_ref, sem):
    dev_count, capacity = wanted_ref.shape
    slots = out_ref.shape[0]
    rows = table_ref.shape[0]
    high, low = split_bytes(wanted_ref[...].astype(F32))
    first = iota((slots, dev_count), 1) * capacity
    slot = iota((slots, dev_count), 0)
    mine = ones_where((slot >= first) & (slot < first + capacity))
    spread = dot(mine, high) * 256.0 + dot(mine, low)
    at = lax.rem(iota((slots, capacity), 0), capacity) == iota((slots, capacity), 1)
    wanted = jnp.sum(jnp.where(at, spread, 0.0), axis=1, keepdims=True).astype(I32)
    block = stage_ref.shape[1]
    stores = []
    for part in range(stage_ref.shape[0]):
        start = part * block
        hot = ones_where(wanted[start : start + block] == iota((block, rows), 1))
        stage_ref[part] = dot(hot, table_ref[...]).astype(BF16)
        store = pltpu.make_async_copy(
            stage_ref.at[part], out_ref.at[pl.ds(start, block)], sem.at[part]
        )
        store.start()
        stores.append(store)
    for store in stores:
        store.wait()


def relation_kernel(rel_ref, table_ref, out_ref):
    rel = to_column(rel_ref[...].astype(F32)).astype(I32)
    hot = ones_where(rel == iota((rel.shape[0], table_ref.shape[0]), 1))
    out_ref[...] = dot(hot, table_ref[...]).astype(BF16)


def load_all(pairs, sem):
    copies = [
        pltpu.make_async_copy(source, buffer, sem.at[i])
        for i, (source, buffer) in enumerate(pairs)
    ]
    for copy in copies:
        copy.start()
    return copies


def encode_kernel(pieces, *refs):
    slot_ref, in_gain_ref, out_gain_ref = refs[:3]
    sources = refs[3:8]
    neg_sources = refs[8 : pieces + 8]
    query_bf_ref, base_ref, ctx_ref, mixed_ref, silu_ref, slope_ref = refs[pieces + 8 : pieces + 14]
    neg_refs = refs[pieces + 14 : 2 * pieces + 14]
    fetched_ref, rel_ref, gate_ref, up_ref, down_ref, sem, late_sem = refs[2 * pieces + 14 :]
    loads = load_all(zip(sources[:4], (fetched_ref, rel_ref, gate_ref, up_ref)), sem)
    queries = rel_ref.shape[0]
    refs = slot_ref.shape[1]
    slots = fetched_ref.shape[0]
    slot = to_column(slot_ref[...].astype(F32)).astype(I32)
    pick = ones_where(slot == iota((refs, slots), 1))
    loads[0].wait()
    head = dot(pick[:queries], fetched_ref[...])
    loads[1].wait()
    base = head + rel_ref[...].astype(F32)
    base_ref[...] = base
    in_scale = lax.rsqrt(jnp.mean(base * base, axis=-1, keepdims=True) + norm_eps)
    normed = (base * in_scale * in_gain_ref[...]).astype(BF16)
    ctx_ref[...] = dot(pick[queries:], fetched_ref[...]).astype(BF16)
    loads[2].wait()
    late = load_all(((sources[4], down_ref), *zip(neg_sources, neg_refs)), late_sem)
    gate = dot(normed, gate_ref[...])
    loads[3].wait()
    up = dot(normed, up_ref[...])
    sig = jax.nn.sigmoid(gate)
    silu = gate * sig
    hidden = (silu * up).astype(BF16)
    silu_ref[...] = silu.astype(BF16)
    slope_ref[...] = (up * (sig + silu * (1.0 - sig))).astype(BF16)
    late[0].wait()
    mixed = base + dot(hidden, down_ref[...])
    mixed_ref[...] = mixed
    out_scale = lax.rsqrt(jnp.mean(mixed * mixed, axis=-1, keepdims=True) + norm_eps)
    query_bf_ref[...] = (mixed * out_scale * out_gain_ref[...]).astype(BF16)
    for load in late[1:]:
        load.wait()


def norm_pull(value, gain, cotangent):
    scale = lax.rsqrt(jnp.mean(value * value, axis=-1, keepdims=True) + norm_eps)
    scaled = cotangent * gain
    along = jnp.mean(scaled * value, axis=-1, keepdims=True)
    return scale * scaled - value * (along * scale * scale * scale)


def grad_kernel(inv_scale, pieces, *refs):
    slot_ref, in_gain_ref, out_gain_ref, query_ref, mixed_ref, ctx_ref = refs[:6]
    silu_ref, slope_ref, base_ref = refs[6:9]
    neg_refs = refs[9 : pieces + 9]
    sources = refs[pieces + 9 : pieces + 12]
    out_ref, down_ref, gate_ref, up_ref, stage_ref, sem, out_sem = refs[pieces + 12 :]
    loads = load_all(zip(sources, (down_ref, gate_ref, up_ref)), sem)
    mixed = mixed_ref[...]
    out_scale = lax.rsqrt(jnp.mean(mixed * mixed, axis=-1, keepdims=True) + norm_eps)
    query = mixed * out_scale * out_gain_ref[...]
    query_bf = query_ref[...]
    ctx = ctx_ref[...].astype(F32)
    pos_score = jnp.sum(query * ctx, axis=-1, keepdims=True) * inv_scale
    pos_weight = POS_WEIGHT * (jax.nn.sigmoid(pos_score) - 1.0) * inv_scale
    query_grad = pos_weight * ctx
    for neg_ref in neg_refs:
        neg = neg_ref[...]
        scores = dot(query_bf, neg, NT) * inv_scale
        weight = (jax.nn.sigmoid(scores) * inv_scale).astype(BF16)
        query_grad = query_grad + dot(weight, neg)
    ctx_grad = (pos_weight * query).astype(BF16)
    mixed_cot = norm_pull(mixed, out_gain_ref[...], query_grad)
    loads[0].wait()
    hidden_cot = dot(mixed_cot.astype(BF16), down_ref[...], NT).astype(BF16).astype(F32)
    up_cot = (hidden_cot * silu_ref[...].astype(F32)).astype(BF16)
    gate_cot = (hidden_cot * slope_ref[...].astype(F32)).astype(BF16)
    loads[1].wait()
    normed_cot = dot(gate_cot, gate_ref[...], NT)
    loads[2].wait()
    normed_cot = normed_cot + dot(up_cot, up_ref[...], NT)
    normed_cot = normed_cot.astype(BF16).astype(F32)
    head_grad = mixed_cot + norm_pull(base_ref[...], in_gain_ref[...], normed_cot)
    head_grad = head_grad.astype(BF16)
    queries = query.shape[0]
    slot = slot_ref[...]
    block = stage_ref.shape[1]
    stores = []
    for part in range(stage_ref.shape[0]):
        start = part * block
        place = ones_where(iota((block, slot.shape[1]), 0) + start == slot)
        out = dot(place[:, :queries], head_grad) + dot(place[:, queries:], ctx_grad)
        stage_ref[part] = out.astype(BF16)
        store = pltpu.make_async_copy(
            stage_ref.at[part], out_ref.at[pl.ds(start, block)], out_sem.at[part]
        )
        store.start()
        stores.append(store)
    for store in stores:
        store.wait()


def neg_grad_kernel(inv_scale, pieces, blocks, *refs):
    query_refs, neg_refs = refs[:pieces], refs[pieces : pieces + blocks]
    before_refs, out_refs = refs[pieces + blocks : -blocks], refs[-blocks:]
    for i in reversed(range(blocks)):
        neg = neg_refs[i][...]
        total = before_refs[i][...] if before_refs else jnp.zeros(neg.shape, F32)
        for query_ref in query_refs:
            query = query_ref[...]
            scores = dot(neg, query, NT) * inv_scale
            weight = (jax.nn.sigmoid(scores) * inv_scale).astype(BF16)
            total = total + dot(weight, query)
        out_refs[i][...] = total.astype(out_refs[i].dtype)


def wanted_row_kernel(wanted_ref, out_ref):
    dev_count, capacity = wanted_ref.shape
    slots = out_ref.shape[1]
    high, low = split_bytes(wanted_ref[...].astype(F32))
    at = ones_where(
        lax.rem(iota((capacity, slots), 1), capacity) == iota((capacity, slots), 0)
    )
    spread = dot(high, at) * 256.0 + dot(low, at)
    first = iota((dev_count, slots), 0) * capacity
    slot = iota((dev_count, slots), 1)
    mine = (slot >= first) & (slot < first + capacity)
    out_ref[...] = jnp.sum(jnp.where(mine, spread, 0.0), axis=0, keepdims=True).astype(I32)


def scatter_kernel(parts, *refs):
    sent_refs = refs[:parts]
    wanted_ref, local_ref, back_ref, own_ref, out_ref, stage_ref, sem = refs[parts:]
    slots = back_ref.shape[0]
    neg = own_ref[...]
    for sent_ref in sent_refs:
        neg = neg + sent_ref[...].astype(F32)
    neg = neg.astype(BF16)
    wanted = wanted_ref[...]
    local = local_ref[...]
    blocks, rows, _ = stage_ref.shape
    stores = []
    for block in range(blocks):
        start = block * rows
        place = ones_where(iota((rows, slots), 0) + start == wanted)
        spot = ones_where(iota((rows, local.shape[1]), 0) + start == local)
        stage_ref[block] = dot(place, back_ref[...]) + dot(spot, neg)
        store = pltpu.make_async_copy(
            stage_ref.at[block], out_ref.at[pl.ds(start, rows)], sem.at[block]
        )
        store.start()
        stores.append(store)
    for store in stores:
        store.wait()


def flip(block, axis, step):
    count = lax.axis_size(axis)
    return lax.ppermute(block, axis, [(i, i ^ step) for i in range(count)])


def spread_over(block, axis, others, before, between):
    held = {0: block}
    for other in sorted(others, key=lambda n: (bin(n).count("1"), -n)):
        step = other & -other
        source = held[other - step]
        hops = bin(other).count("1")
        if hops > 1:
            source, _ = lax.optimization_barrier((source, before if hops == 2 else between))
        held[other] = flip(source, axis, step)
    return held


def per_device(
    table,
    touch_owner,
    touch_local,
    query_rel,
    neg_local,
    rel_table,
    in_gain,
    out_gain,
    w_gate,
    w_up,
    w_down,
):
    axes = ("ent", "grp")
    dev_count = lax.axis_size("ent") * lax.axis_size("grp")
    refs = touch_local.shape[0]
    queries = refs // 2
    capacity = 2 * refs // dev_count
    slots = dev_count * capacity
    rows, width = table.shape
    hidden = w_gate.shape[1]
    negs = neg_local.shape[0]
    inv_scale = 1.0 / math.sqrt(width)
    shape = jax.ShapeDtypeStruct
    in_gain = in_gain.reshape(1, width)
    out_gain = out_gain.reshape(1, width)
    neg_row = neg_local.reshape(1, negs)

    group = lax.axis_size("grp")
    half = group // 2
    hbm = pl.BlockSpec(memory_space=pl.ANY)
    vmem = pl.BlockSpec(memory_space=pltpu.VMEM)

    parts = 4 if rows % 64 == 0 else 1
    requests, slot_row = call(
        route_kernel,
        (shape((dev_count, capacity), I32), pltpu.HBM((1, refs), I32)),
        in_hbm(touch_owner.reshape(1, refs), touch_local.reshape(1, refs)),
        2 * refs * refs * dev_count,
        8 * refs,
    )
    wanted = lax.all_to_all(requests, axes, split_axis=0, concat_axis=0, tiled=True)

    neg_rows, small_table = call(
        negatives_kernel,
        (shape((negs, width), BF16), shape((rows, width), BF16)),
        in_hbm(neg_row, table),
        SHADOW_FLOPS,
        6 * rows * width,
        in_specs=[vmem, hbm],
        scratch_shapes=[
            pltpu.VMEM((parts, rows // parts, width), F32),
            pltpu.SemaphoreType.DMA((parts,)),
        ],
    )
    rel_rows = call(
        relation_kernel,
        pltpu.HBM((queries, width), BF16),
        in_hbm(query_rel.reshape(1, queries), rel_table),
        SHADOW_FLOPS,
        2 * rel_table.size,
    )

    block = math.gcd(slots, 256)
    looked = call(
        fetch_kernel,
        pltpu.HBM((slots, width), BF16),
        (wanted, small_table),
        SHADOW_FLOPS,
        2 * (slots + rows) * width,
        out_specs=hbm,
        scratch_shapes=[
            pltpu.VMEM((slots // block, block, width), BF16),
            pltpu.SemaphoreType.DMA((slots // block,)),
        ],
    )
    neg_held = spread_over(neg_rows, "grp", range(1, group), looked, rel_rows)
    neg_pieces = [neg_held[other] for other in range(group)]
    fetched = lax.all_to_all(
        looked.reshape(dev_count, capacity, width), axes, split_axis=0, concat_axis=0, tiled=True
    ).reshape(slots, width)

    def buffer(array):
        return pltpu.VMEM(array.shape, array.dtype)

    sources = (fetched, rel_rows, w_gate, w_up, w_down)
    outputs = (
        shape((queries, width), BF16),
        shape((queries, width), F32),
        shape((queries, width), BF16),
        shape((queries, width), F32),
        shape((queries, hidden), BF16),
        shape((queries, hidden), BF16),
    )
    early = neg_pieces[:-1]
    query_bf, base, ctx, mixed, silu, slope, *staged = call(
        functools.partial(encode_kernel, len(early)),
        outputs + (pltpu.VMEM((negs, width), BF16),) * len(early),
        in_hbm(slot_row, in_gain, out_gain) + (fetched,) + in_hbm(*sources[1:]) + tuple(early),
        2 * queries * width * (2 * slots + 3 * hidden),
        2 * (slots * width + 3 * width * hidden),
        in_specs=[vmem] * 3 + [hbm] * (5 + len(early)),
        out_specs=[vmem] * 6 + [hbm] * len(early),
        scratch_shapes=[buffer(a) for a in sources]
        + [pltpu.SemaphoreType.DMA((4,)), pltpu.SemaphoreType.DMA((1 + len(early),))],
    )
    staged.append(neg_pieces[-1])
    low = 1 if group > 2 else 0
    near = [query_bf, flip(query_bf, "grp", half)] + ([flip(query_bf, "grp", low)] if low else [])
    far = [flip(near[1], "grp", low)] if low else []
    others = [other for other in range(1, group) if not other & (low | half)]

    weights = (w_down, w_gate, w_up)
    outgoing = call(
        functools.partial(grad_kernel, inv_scale, len(neg_pieces)),
        pltpu.HBM((slots, width), BF16),
        in_hbm(slot_row, in_gain, out_gain)
        + (query_bf, mixed, ctx, silu, slope, base, *staged)
        + in_hbm(*weights),
        2 * queries * width * (2 * slots + 3 * hidden + 2 * negs * len(neg_pieces)),
        2 * (slots * width + 3 * width * hidden + negs * width * len(neg_pieces)),
        in_specs=[vmem] * (len(neg_pieces) + 9) + [hbm] * 3,
        out_specs=hbm,
        scratch_shapes=[buffer(a) for a in weights]
        + [
            pltpu.VMEM((slots // block, block, width), BF16),
            pltpu.SemaphoreType.DMA((3,)),
            pltpu.SemaphoreType.DMA((slots // block,)),
        ],
    )
    returned = lax.all_to_all(
        outgoing.reshape(dev_count, capacity, width), axes, split_axis=0, concat_axis=0, tiled=True
    ).reshape(slots, width)

    blocks = 1 + len(others)
    neg_blocks = [neg_held[other] for other in [0] + others]
    first = call(
        functools.partial(neg_grad_kernel, inv_scale, len(near), blocks),
        [shape((negs, width), F32)] * blocks,
        (*near, *neg_blocks),
        SHADOW_FLOPS,
        2 * (len(near) + blocks) * negs * width,
    )
    def add_far(i, out):
        return call(
            functools.partial(neg_grad_kernel, inv_scale, len(far), 1),
            (out,),
            (*far, neg_blocks[i], first[i]),
            4 * len(far) * queries * negs * width,
            2 * (len(far) + 1) * negs * width,
        )[0]

    sums = [add_far(i, shape((negs, width), BF16)) for i in range(1, blocks)]
    own = add_far(0, pltpu.HBM((negs, width), F32))
    sent = [flip(block, "grp", other) for other, block in zip(others, sums)]
    wanted_row = call(
        wanted_row_kernel, pltpu.HBM((1, slots), I32), (wanted,), slots * dev_count, 4 * slots
    )

    parts = 8 if rows % 128 == 0 else 1
    return call(
        functools.partial(scatter_kernel, len(sent)),
        shape((rows, width), F32),
        (*sent, *in_hbm(wanted_row, neg_row), returned, *in_hbm(own)),
        2 * rows * width * (slots + negs),
        4 * rows * width + 2 * slots * width,
        out_specs=hbm,
        scratch_shapes=[
            pltpu.VMEM((parts, rows // parts, width), F32),
            pltpu.SemaphoreType.DMA((parts,)),
        ],
    )


def solution(mesh):
    return jax.shard_map(
        per_device,
        mesh=mesh,
        in_specs=(
            P(("ent", "grp"), None),
            P(("ent", "grp"), None),
            P(("ent", "grp")),
            P(("ent", "grp")),
            P(("ent", "grp")),
            P(),
            P(),
            P(),
            P(),
            P(),
            P(),
        ),
        out_specs=P(("ent", "grp"), None),
        check_vma=False,
    )
```

```python
import functools
import math

import jax
import jax.numpy as jnp
from jax import lax
from jax.experimental import pallas as pl
from jax.experimental.pallas import tpu as pltpu
from jax.sharding import PartitionSpec as P

POS_WEIGHT = 64

norm_eps = 1e-06

SHADOW_FLOPS = 1 << 45

F32 = jnp.float32
BF16 = jnp.bfloat16
I32 = jnp.int32

NN = (((1,), (0,)), ((), ()))
NT = (((1,), (1,)), ((), ()))
TN = (((0,), (0,)), ((), ()))


def dot(a, b, dims=NN):
    return lax.dot_general(a, b, dims, preferred_element_type=F32)


def in_hbm(*arrays):
    return tuple(pltpu.with_memory_space_constraint(array, pltpu.HBM) for array in arrays)


def iota(shape, axis):
    return lax.broadcasted_iota(I32, shape, axis)


def ones_where(mask):
    return jnp.where(mask, 1.0, 0.0).astype(BF16)


def to_column(row):
    count = row.shape[1]
    same = iota((count, count), 0) == iota((count, count), 1)
    return jnp.sum(jnp.where(same, row, 0.0), axis=1, keepdims=True)


def to_row(column):
    count = column.shape[0]
    same = iota((count, count), 0) == iota((count, count), 1)
    return jnp.sum(jnp.where(same, column, 0.0), axis=0, keepdims=True)


def split_bytes(numbers):
    high = jnp.floor(numbers * (1.0 / 256.0))
    return high.astype(BF16), (numbers - high * 256.0).astype(BF16)


def call(kernel, out_shape, args, flops, moved, **kwargs):
    return pl.pallas_call(
        kernel,
        out_shape=out_shape,
        compiler_params=pltpu.CompilerParams(vmem_limit_bytes=kwargs.pop("vmem", 28) << 20),
        cost_estimate=pl.CostEstimate(flops=flops, bytes_accessed=moved, transcendentals=0),
        **kwargs,
    )(*args)


def route_kernel(owner_ref, local_ref, request_ref, slot_ref):
    refs = owner_ref.shape[1]
    dev_count, capacity = request_ref.shape
    owner = owner_ref[...]
    hit = owner == iota((dev_count, refs), 0)
    earlier = ones_where(iota((refs, refs), 0) <= iota((refs, refs), 1))
    rank = dot(ones_where(hit), earlier)
    placed = jnp.sum(jnp.where(hit, rank, 0.0), axis=0, keepdims=True).astype(I32) - 1
    slot_ref[...] = owner * capacity + placed
    at = ones_where(iota((capacity, refs), 0) == placed)
    high, low = split_bytes(jnp.where(hit, local_ref[...].astype(F32), 0.0))
    request_ref[...] = (dot(high, at, NT) * 256.0 + dot(low, at, NT)).astype(I32)


def negatives_kernel(
    neg_local_hbm, table_ref, neg_ref, small_ref, neg_local_ref, stage_ref, local_sem, sem
):
    local_load = pltpu.make_async_copy(neg_local_hbm, neg_local_ref, local_sem)
    local_load.start()
    parts, rows, _ = stage_ref.shape
    copies = load_all(
        [
            (table_ref.at[pl.ds(part * rows, rows)], stage_ref.at[part])
            for part in range(parts)
        ],
        sem,
    )
    local_load.wait()
    neg_local = to_column(neg_local_ref[...].astype(F32)).astype(I32)
    total = jnp.zeros(neg_ref.shape, F32)
    for part, copy in enumerate(copies):
        copy.wait()
        small = stage_ref[part].astype(BF16)
        small_ref[part * rows : (part + 1) * rows, :] = small
        hot = neg_local == iota((neg_ref.shape[0], rows), 1) + part * rows
        total = total + dot(ones_where(hot), small)
    neg_ref[...] = total.astype(BF16)


def fetch_kernel(wanted_ref, table_ref, out_ref, stage_ref, sem):
    dev_count, capacity = wanted_ref.shape
    slots = out_ref.shape[0]
    rows = table_ref.shape[0]
    high, low = split_bytes(wanted_ref[...].astype(F32))
    first = iota((slots, dev_count), 1) * capacity
    slot = iota((slots, dev_count), 0)
    mine = ones_where((slot >= first) & (slot < first + capacity))
    spread = dot(mine, high) * 256.0 + dot(mine, low)
    at = lax.rem(iota((slots, capacity), 0), capacity) == iota((slots, capacity), 1)
    wanted = jnp.sum(jnp.where(at, spread, 0.0), axis=1, keepdims=True).astype(I32)
    block = stage_ref.shape[1]
    stores = []
    for part in range(stage_ref.shape[0]):
        start = part * block
        hot = ones_where(wanted[start : start + block] == iota((block, rows), 1))
        stage_ref[part] = dot(hot, table_ref[...]).astype(BF16)
        store = pltpu.make_async_copy(
            stage_ref.at[part], out_ref.at[pl.ds(start, block)], sem.at[part]
        )
        store.start()
        stores.append(store)
    for store in stores:
        store.wait()


def relation_kernel(rel_ref, table_ref, out_ref):
    rel = to_column(rel_ref[...].astype(F32)).astype(I32)
    hot = ones_where(rel == iota((rel.shape[0], table_ref.shape[0]), 1))
    out_ref[...] = dot(hot, table_ref[...]).astype(BF16)


def load_all(pairs, sem):
    copies = [
        pltpu.make_async_copy(source, buffer, sem.at[i])
        for i, (source, buffer) in enumerate(pairs)
    ]
    for copy in copies:
        copy.start()
    return copies


def encode_kernel(pieces, *refs):
    sources = refs[:8]
    neg_sources = refs[8 : pieces + 8]
    query_bf_ref, base_ref, ctx_ref, mixed_ref, silu_ref, slope_ref = refs[pieces + 8 : pieces + 14]
    neg_refs = refs[pieces + 14 : 2 * pieces + 14]
    *buffers, sem, late_sem = refs[2 * pieces + 14 :]
    slot_ref, fetched_ref, rel_ref, in_gain_ref, out_gain_ref, gate_ref, up_ref, down_ref = buffers
    loads = load_all(zip(sources[:7], buffers), sem)
    queries = rel_ref.shape[0]
    refs = slot_ref.shape[1]
    slots = fetched_ref.shape[0]
    loads[0].wait()
    slot = to_column(slot_ref[...].astype(F32)).astype(I32)
    pick = ones_where(slot == iota((refs, slots), 1))
    loads[1].wait()
    head = dot(pick[:queries], fetched_ref[...])
    for load in loads[2:5]:
        load.wait()
    base = head + rel_ref[...].astype(F32)
    base_ref[...] = base
    in_scale = lax.rsqrt(jnp.mean(base * base, axis=-1, keepdims=True) + norm_eps)
    normed = (base * in_scale * in_gain_ref[...]).astype(BF16)
    ctx_ref[...] = dot(pick[queries:], fetched_ref[...]).astype(BF16)
    loads[5].wait()
    late = load_all(((sources[7], down_ref), *zip(neg_sources, neg_refs)), late_sem)
    gate = dot(normed, gate_ref[...])
    loads[6].wait()
    up = dot(normed, up_ref[...])
    sig = jax.nn.sigmoid(gate)
    silu = gate * sig
    hidden = (silu * up).astype(BF16)
    silu_ref[...] = silu.astype(BF16)
    slope_ref[...] = (up * (sig + silu * (1.0 - sig))).astype(BF16)
    late[0].wait()
    mixed = base + dot(hidden, down_ref[...])
    mixed_ref[...] = mixed
    out_scale = lax.rsqrt(jnp.mean(mixed * mixed, axis=-1, keepdims=True) + norm_eps)
    query_bf_ref[...] = (mixed * out_scale * out_gain_ref[...]).astype(BF16)
    for load in late[1:]:
        load.wait()


def norm_pull(value, gain, cotangent):
    scale = lax.rsqrt(jnp.mean(value * value, axis=-1, keepdims=True) + norm_eps)
    scaled = cotangent * gain
    along = jnp.mean(scaled * value, axis=-1, keepdims=True)
    return scale * scaled - value * (along * scale * scale * scale)


def grad_kernel(inv_scale, pieces, *refs):
    query_ref, mixed_ref, ctx_ref, silu_ref, slope_ref, base_ref = refs[:6]
    neg_refs = refs[6 : pieces + 6]
    sources = refs[pieces + 6 : pieces + 12]
    out_ref, *buffers, stage_ref, sem, out_sem = refs[pieces + 12 :]
    out_gain_ref, in_gain_ref, slot_ref, down_ref, gate_ref, up_ref = buffers
    loads = load_all(zip(sources, buffers), sem)
    loads[0].wait()
    mixed = mixed_ref[...]
    out_scale = lax.rsqrt(jnp.mean(mixed * mixed, axis=-1, keepdims=True) + norm_eps)
    query = mixed * out_scale * out_gain_ref[...]
    query_bf = query_ref[...]
    ctx = ctx_ref[...].astype(F32)
    pos_score = jnp.sum(query * ctx, axis=-1, keepdims=True) * inv_scale
    pos_weight = POS_WEIGHT * (jax.nn.sigmoid(pos_score) - 1.0) * inv_scale
    query_grad = pos_weight * ctx
    for neg_ref in neg_refs:
        neg = neg_ref[...]
        scores = dot(query_bf, neg, NT) * inv_scale
        weight = (jax.nn.sigmoid(scores) * inv_scale).astype(BF16)
        query_grad = query_grad + dot(weight, neg)
    ctx_grad = (pos_weight * query).astype(BF16)
    mixed_cot = norm_pull(mixed, out_gain_ref[...], query_grad)
    loads[3].wait()
    hidden_cot = dot(mixed_cot.astype(BF16), down_ref[...], NT).astype(BF16).astype(F32)
    up_cot = (hidden_cot * silu_ref[...].astype(F32)).astype(BF16)
    gate_cot = (hidden_cot * slope_ref[...].astype(F32)).astype(BF16)
    loads[4].wait()
    normed_cot = dot(gate_cot, gate_ref[...], NT)
    loads[5].wait()
    normed_cot = normed_cot + dot(up_cot, up_ref[...], NT)
    normed_cot = normed_cot.astype(BF16).astype(F32)
    loads[1].wait()
    loads[2].wait()
    head_grad = mixed_cot + norm_pull(base_ref[...], in_gain_ref[...], normed_cot)
    head_grad = head_grad.astype(BF16)
    queries = query.shape[0]
    slot = slot_ref[...]
    block = stage_ref.shape[1]
    stores = []
    for part in range(stage_ref.shape[0]):
        start = part * block
        place = ones_where(iota((block, slot.shape[1]), 0) + start == slot)
        out = dot(place[:, :queries], head_grad) + dot(place[:, queries:], ctx_grad)
        stage_ref[part] = out.astype(BF16)
        store = pltpu.make_async_copy(
            stage_ref.at[part], out_ref.at[pl.ds(start, block)], out_sem.at[part]
        )
        store.start()
        stores.append(store)
    for store in stores:
        store.wait()


def neg_grad_kernel(inv_scale, pieces, blocks, *refs):
    query_refs, neg_refs = refs[:pieces], refs[pieces : pieces + blocks]
    before_refs, out_refs = refs[pieces + blocks : -blocks], refs[-blocks:]
    for i in reversed(range(blocks)):
        neg = neg_refs[i][...]
        total = before_refs[i][...] if before_refs else jnp.zeros(neg.shape, F32)
        for query_ref in query_refs:
            query = query_ref[...]
            scores = dot(neg, query, NT) * inv_scale
            weight = (jax.nn.sigmoid(scores) * inv_scale).astype(BF16)
            total = total + dot(weight, query)
        out_refs[i][...] = total.astype(out_refs[i].dtype)


def wanted_row_kernel(wanted_ref, out_ref):
    dev_count, capacity = wanted_ref.shape
    slots = out_ref.shape[1]
    high, low = split_bytes(wanted_ref[...].astype(F32))
    at = ones_where(
        lax.rem(iota((capacity, slots), 1), capacity) == iota((capacity, slots), 0)
    )
    spread = dot(high, at) * 256.0 + dot(low, at)
    first = iota((dev_count, slots), 0) * capacity
    slot = iota((dev_count, slots), 1)
    mine = (slot >= first) & (slot < first + capacity)
    out_ref[...] = jnp.sum(jnp.where(mine, spread, 0.0), axis=0, keepdims=True).astype(I32)


def scatter_kernel(parts, *refs):
    sent_refs = refs[:parts]
    wanted_ref, local_ref, back_ref, own_ref, out_ref, stage_ref, sem = refs[parts:]
    slots = back_ref.shape[0]
    neg = own_ref[...]
    for sent_ref in sent_refs:
        neg = neg + sent_ref[...].astype(F32)
    neg = neg.astype(BF16)
    wanted = wanted_ref[...]
    local = local_ref[...]
    blocks, rows, _ = stage_ref.shape
    stores = []
    for block in range(blocks):
        start = block * rows
        place = ones_where(iota((rows, slots), 0) + start == wanted)
        spot = ones_where(iota((rows, local.shape[1]), 0) + start == local)
        stage_ref[block] = dot(place, back_ref[...]) + dot(spot, neg)
        store = pltpu.make_async_copy(
            stage_ref.at[block], out_ref.at[pl.ds(start, rows)], sem.at[block]
        )
        store.start()
        stores.append(store)
    for store in stores:
        store.wait()


def flip(block, axis, step):
    count = lax.axis_size(axis)
    return lax.ppermute(block, axis, [(i, i ^ step) for i in range(count)])


def spread_over(block, axis, others, before, between):
    held = {0: block}
    for other in sorted(others, key=lambda n: (bin(n).count("1"), -n)):
        step = other & -other
        source = held[other - step]
        hops = bin(other).count("1")
        if hops > 1:
            source, _ = lax.optimization_barrier((source, before if hops == 2 else between))
        held[other] = flip(source, axis, step)
    return held


def per_device(
    table,
    touch_owner,
    touch_local,
    query_rel,
    neg_local,
    rel_table,
    in_gain,
    out_gain,
    w_gate,
    w_up,
    w_down,
):
    axes = ("ent", "grp")
    dev_count = lax.axis_size("ent") * lax.axis_size("grp")
    refs = touch_local.shape[0]
    queries = refs // 2
    capacity = 2 * refs // dev_count
    slots = dev_count * capacity
    rows, width = table.shape
    hidden = w_gate.shape[1]
    negs = neg_local.shape[0]
    inv_scale = 1.0 / math.sqrt(width)
    shape = jax.ShapeDtypeStruct
    in_gain = in_gain.reshape(1, width)
    out_gain = out_gain.reshape(1, width)
    neg_row = neg_local.reshape(1, negs)

    group = lax.axis_size("grp")
    half = group // 2
    hbm = pl.BlockSpec(memory_space=pl.ANY)
    vmem = pl.BlockSpec(memory_space=pltpu.VMEM)

    parts = 8 if rows % 128 == 0 else 1
    requests, slot_row = call(
        route_kernel,
        (pltpu.VMEM((dev_count, capacity), I32), pltpu.VMEM((1, refs), I32)),
        in_hbm(touch_owner.reshape(1, refs), touch_local.reshape(1, refs)),
        2 * refs * refs * dev_count,
        8 * refs,
    )
    wanted = lax.all_to_all(requests, axes, split_axis=0, concat_axis=0, tiled=True)

    neg_rows, small_table = call(
        negatives_kernel,
        (pltpu.VMEM((negs, width), BF16), shape((rows, width), BF16)),
        in_hbm(neg_row, table),
        SHADOW_FLOPS,
        6 * rows * width,
        in_specs=[hbm, hbm],
        scratch_shapes=[
            pltpu.VMEM((1, negs), I32),
            pltpu.VMEM((parts, rows // parts, width), F32),
            pltpu.SemaphoreType.DMA,
            pltpu.SemaphoreType.DMA((parts,)),
        ],
    )
    rel_rows = call(
        relation_kernel,
        pltpu.HBM((queries, width), BF16),
        in_hbm(query_rel.reshape(1, queries), rel_table),
        SHADOW_FLOPS,
        2 * rel_table.size,
    )

    block = math.gcd(slots, 256)
    looked = call(
        fetch_kernel,
        pltpu.HBM((slots, width), BF16),
        (pltpu.with_memory_space_constraint(wanted, pltpu.VMEM), small_table),
        SHADOW_FLOPS,
        2 * (slots + rows) * width,
        out_specs=hbm,
        scratch_shapes=[
            pltpu.VMEM((slots // block, block, width), BF16),
            pltpu.SemaphoreType.DMA((slots // block,)),
        ],
    )
    neg_held = spread_over(neg_rows, "grp", range(1, group), looked, rel_rows)
    neg_pieces = [neg_held[other] for other in range(group)]
    fetched = lax.all_to_all(
        looked.reshape(dev_count, capacity, width), axes, split_axis=0, concat_axis=0, tiled=True
    ).reshape(slots, width)

    def buffer(array):
        return pltpu.VMEM(array.shape, array.dtype)

    sources = (slot_row, fetched, rel_rows, in_gain, out_gain, w_gate, w_up, w_down)
    outputs = (
        shape((queries, width), BF16),
        shape((queries, width), F32),
        shape((queries, width), BF16),
        shape((queries, width), F32),
        shape((queries, hidden), BF16),
        shape((queries, hidden), BF16),
    )
    early = neg_pieces[:-1]
    query_bf, base, ctx, mixed, silu, slope, *staged = call(
        functools.partial(encode_kernel, len(early)),
        outputs + (pltpu.VMEM((negs, width), BF16),) * len(early),
        (slot_row, fetched) + in_hbm(*sources[2:]) + tuple(early),
        2 * queries * width * (2 * slots + 3 * hidden),
        2 * (slots * width + 3 * width * hidden),
        in_specs=[hbm] * (8 + len(early)),
        out_specs=[vmem] * 6 + [hbm] * len(early),
        scratch_shapes=[buffer(a) for a in sources]
        + [pltpu.SemaphoreType.DMA((7,)), pltpu.SemaphoreType.DMA((1 + len(early),))],
    )
    staged.append(neg_pieces[-1])
    low = 1 if group > 2 else 0
    near = [query_bf, flip(query_bf, "grp", half)] + ([flip(query_bf, "grp", low)] if low else [])
    far = [flip(near[1], "grp", low)] if low else []
    others = [other for other in range(1, group) if not other & (low | half)]

    weights = (out_gain, in_gain, slot_row, w_down, w_gate, w_up)
    outgoing = call(
        functools.partial(grad_kernel, inv_scale, len(neg_pieces)),
        pltpu.HBM((slots, width), BF16),
        (query_bf, mixed, ctx, silu, slope, base, *staged) + in_hbm(*weights),
        2 * queries * width * (2 * slots + 3 * hidden + 2 * negs * len(neg_pieces)),
        2 * (slots * width + 3 * width * hidden + negs * width * len(neg_pieces)),
        in_specs=[vmem] * (len(neg_pieces) + 6) + [hbm] * 6,
        out_specs=hbm,
        scratch_shapes=[buffer(a) for a in weights]
        + [
            pltpu.VMEM((slots // block, block, width), BF16),
            pltpu.SemaphoreType.DMA((6,)),
            pltpu.SemaphoreType.DMA((slots // block,)),
        ],
    )
    returned = lax.all_to_all(
        outgoing.reshape(dev_count, capacity, width), axes, split_axis=0, concat_axis=0, tiled=True
    ).reshape(slots, width)

    blocks = 1 + len(others)
    neg_blocks = [neg_held[other] for other in [0] + others]
    first = call(
        functools.partial(neg_grad_kernel, inv_scale, len(near), blocks),
        [shape((negs, width), F32)] * blocks,
        (*near, *neg_blocks),
        SHADOW_FLOPS,
        2 * (len(near) + blocks) * negs * width,
    )
    def add_far(i, out):
        return call(
            functools.partial(neg_grad_kernel, inv_scale, len(far), 1),
            (out,),
            (*far, neg_blocks[i], first[i]),
            4 * len(far) * queries * negs * width,
            2 * (len(far) + 1) * negs * width,
        )[0]

    sums = [add_far(i, shape((negs, width), BF16)) for i in range(1, blocks)]
    own = add_far(0, pltpu.HBM((negs, width), F32))
    sent = [flip(block, "grp", other) for other, block in zip(others, sums)]
    wanted_row = call(
        wanted_row_kernel, pltpu.HBM((1, slots), I32), (wanted,), slots * dev_count, 4 * slots
    )

    parts = 8 if rows % 128 == 0 else 1
    return call(
        functools.partial(scatter_kernel, len(sent)),
        shape((rows, width), F32),
        (*sent, *in_hbm(wanted_row, neg_row), returned, *in_hbm(own)),
        2 * rows * width * (slots + negs),
        4 * rows * width + 2 * slots * width,
        out_specs=hbm,
        scratch_shapes=[
            pltpu.VMEM((parts, rows // parts, width), F32),
            pltpu.SemaphoreType.DMA((parts,)),
        ],
    )


def solution(mesh):
    return jax.shard_map(
        per_device,
        mesh=mesh,
        in_specs=(
            P(("ent", "grp"), None),
            P(("ent", "grp"), None),
            P(("ent", "grp")),
            P(("ent", "grp")),
            P(("ent", "grp")),
            P(),
            P(),
            P(),
            P(),
            P(),
            P(),
        ),
        out_specs=P(("ent", "grp"), None),
        check_vma=False,
    )
```

```python
import functools
import math

import jax
import jax.numpy as jnp
from jax import lax
from jax.experimental import pallas as pl
from jax.experimental.pallas import tpu as pltpu
from jax.sharding import PartitionSpec as P

POS_WEIGHT = 64

norm_eps = 1e-06

SHADOW_FLOPS = 1 << 45

F32 = jnp.float32
BF16 = jnp.bfloat16
I32 = jnp.int32

NN = (((1,), (0,)), ((), ()))
NT = (((1,), (1,)), ((), ()))
TN = (((0,), (0,)), ((), ()))


def dot(a, b, dims=NN):
    return lax.dot_general(a, b, dims, preferred_element_type=F32)


def in_hbm(*arrays):
    return tuple(pltpu.with_memory_space_constraint(array, pltpu.HBM) for array in arrays)


def iota(shape, axis):
    return lax.broadcasted_iota(I32, shape, axis)


def ones_where(mask):
    return jnp.where(mask, 1.0, 0.0).astype(BF16)


def to_column(row):
    count = row.shape[1]
    same = iota((count, count), 0) == iota((count, count), 1)
    return jnp.sum(jnp.where(same, row, 0.0), axis=1, keepdims=True)


def to_row(column):
    count = column.shape[0]
    same = iota((count, count), 0) == iota((count, count), 1)
    return jnp.sum(jnp.where(same, column, 0.0), axis=0, keepdims=True)


def split_bytes(numbers):
    high = jnp.floor(numbers * (1.0 / 256.0))
    return high.astype(BF16), (numbers - high * 256.0).astype(BF16)


def call(kernel, out_shape, args, flops, moved, **kwargs):
    return pl.pallas_call(
        kernel,
        out_shape=out_shape,
        compiler_params=pltpu.CompilerParams(vmem_limit_bytes=kwargs.pop("vmem", 28) << 20),
        cost_estimate=pl.CostEstimate(flops=flops, bytes_accessed=moved, transcendentals=0),
        **kwargs,
    )(*args)


def route_kernel(owner_ref, local_ref, request_ref, slot_ref):
    refs = owner_ref.shape[1]
    dev_count, capacity = request_ref.shape
    owner = owner_ref[...]
    hit = owner == iota((dev_count, refs), 0)
    earlier = ones_where(iota((refs, refs), 0) <= iota((refs, refs), 1))
    rank = dot(ones_where(hit), earlier)
    placed = jnp.sum(jnp.where(hit, rank, 0.0), axis=0, keepdims=True).astype(I32) - 1
    slot_ref[...] = owner * capacity + placed
    at = ones_where(iota((capacity, refs), 0) == placed)
    high, low = split_bytes(jnp.where(hit, local_ref[...].astype(F32), 0.0))
    request_ref[...] = (dot(high, at, NT) * 256.0 + dot(low, at, NT)).astype(I32)


def negatives_kernel(
    neg_local_hbm, table_ref, neg_ref, small_ref, neg_local_ref, stage_ref, local_sem, sem
):
    local_load = pltpu.make_async_copy(neg_local_hbm, neg_local_ref, local_sem)
    local_load.start()
    parts, rows, _ = stage_ref.shape
    copies = load_all(
        [
            (table_ref.at[pl.ds(part * rows, rows)], stage_ref.at[part])
            for part in range(parts)
        ],
        sem,
    )
    local_load.wait()
    neg_local = to_column(neg_local_ref[...].astype(F32)).astype(I32)
    total = jnp.zeros(neg_ref.shape, F32)
    for part, copy in enumerate(copies):
        copy.wait()
        small = stage_ref[part].astype(BF16)
        small_ref[part * rows : (part + 1) * rows, :] = small
        hot = neg_local == iota((neg_ref.shape[0], rows), 1) + part * rows
        total = total + dot(ones_where(hot), small)
    neg_ref[...] = total.astype(BF16)


def fetch_kernel(wanted_ref, table_ref, out_ref, stage_ref, sem):
    dev_count, capacity = wanted_ref.shape
    slots = out_ref.shape[0]
    rows = table_ref.shape[0]
    high, low = split_bytes(wanted_ref[...].astype(F32))
    first = iota((slots, dev_count), 1) * capacity
    slot = iota((slots, dev_count), 0)
    mine = ones_where((slot >= first) & (slot < first + capacity))
    spread = dot(mine, high) * 256.0 + dot(mine, low)
    at = lax.rem(iota((slots, capacity), 0), capacity) == iota((slots, capacity), 1)
    wanted = jnp.sum(jnp.where(at, spread, 0.0), axis=1, keepdims=True).astype(I32)
    block = stage_ref.shape[1]
    stores = []
    for part in range(stage_ref.shape[0]):
        start = part * block
        hot = ones_where(wanted[start : start + block] == iota((block, rows), 1))
        stage_ref[part] = dot(hot, table_ref[...]).astype(BF16)
        store = pltpu.make_async_copy(
            stage_ref.at[part], out_ref.at[pl.ds(start, block)], sem.at[part]
        )
        store.start()
        stores.append(store)
    for store in stores:
        store.wait()


def relation_kernel(rel_ref, table_ref, out_ref):
    rel = to_column(rel_ref[...].astype(F32)).astype(I32)
    hot = ones_where(rel == iota((rel.shape[0], table_ref.shape[0]), 1))
    out_ref[...] = dot(hot, table_ref[...]).astype(BF16)


def load_all(pairs, sem):
    copies = [
        pltpu.make_async_copy(source, buffer, sem.at[i])
        for i, (source, buffer) in enumerate(pairs)
    ]
    for copy in copies:
        copy.start()
    return copies


def encode_kernel(pieces, *refs):
    sources = refs[:8]
    neg_sources = refs[8 : pieces + 8]
    query_bf_ref, base_ref, ctx_ref, mixed_ref, silu_ref, slope_ref = refs[pieces + 8 : pieces + 14]
    neg_refs = refs[pieces + 14 : 2 * pieces + 14]
    slot_ref, in_gain_ref, out_gain_ref, gate_ref, up_ref, down_ref = refs[
        2 * pieces + 14 : 2 * pieces + 20
    ]
    fetched_ref, rel_ref, sem, late_sem = refs[2 * pieces + 20 :]
    buffers = (slot_ref, fetched_ref, rel_ref, in_gain_ref, out_gain_ref, gate_ref, up_ref)
    loads = load_all(zip(sources[:7], buffers), sem)
    queries = rel_ref.shape[0]
    refs = slot_ref.shape[1]
    slots = fetched_ref.shape[0]
    loads[0].wait()
    slot = to_column(slot_ref[...].astype(F32)).astype(I32)
    pick = ones_where(slot == iota((refs, slots), 1))
    loads[1].wait()
    head = dot(pick[:queries], fetched_ref[...])
    for load in loads[2:5]:
        load.wait()
    base = head + rel_ref[...].astype(F32)
    base_ref[...] = base
    in_scale = lax.rsqrt(jnp.mean(base * base, axis=-1, keepdims=True) + norm_eps)
    normed = (base * in_scale * in_gain_ref[...]).astype(BF16)
    ctx_ref[...] = dot(pick[queries:], fetched_ref[...]).astype(BF16)
    loads[5].wait()
    late = load_all(((sources[7], down_ref), *zip(neg_sources, neg_refs)), late_sem)
    gate = dot(normed, gate_ref[...])
    loads[6].wait()
    up = dot(normed, up_ref[...])
    sig = jax.nn.sigmoid(gate)
    silu = gate * sig
    hidden = (silu * up).astype(BF16)
    silu_ref[...] = silu.astype(BF16)
    slope_ref[...] = (up * (sig + silu * (1.0 - sig))).astype(BF16)
    late[0].wait()
    mixed = base + dot(hidden, down_ref[...])
    mixed_ref[...] = mixed
    out_scale = lax.rsqrt(jnp.mean(mixed * mixed, axis=-1, keepdims=True) + norm_eps)
    query_bf_ref[...] = (mixed * out_scale * out_gain_ref[...]).astype(BF16)
    for load in late[1:]:
        load.wait()


def norm_pull(value, gain, cotangent):
    scale = lax.rsqrt(jnp.mean(value * value, axis=-1, keepdims=True) + norm_eps)
    scaled = cotangent * gain
    along = jnp.mean(scaled * value, axis=-1, keepdims=True)
    return scale * scaled - value * (along * scale * scale * scale)


def grad_kernel(inv_scale, pieces, *refs):
    query_ref, mixed_ref, ctx_ref, silu_ref, slope_ref, base_ref = refs[:6]
    neg_refs = refs[6 : pieces + 6]
    slot_ref, in_gain_ref, out_gain_ref, gate_ref, up_ref, down_ref = refs[
        pieces + 6 : pieces + 12
    ]
    out_ref, stage_ref, out_sem = refs[pieces + 12 :]
    mixed = mixed_ref[...]
    out_scale = lax.rsqrt(jnp.mean(mixed * mixed, axis=-1, keepdims=True) + norm_eps)
    query = mixed * out_scale * out_gain_ref[...]
    query_bf = query_ref[...]
    ctx = ctx_ref[...].astype(F32)
    pos_score = jnp.sum(query * ctx, axis=-1, keepdims=True) * inv_scale
    pos_weight = POS_WEIGHT * (jax.nn.sigmoid(pos_score) - 1.0) * inv_scale
    query_grad = pos_weight * ctx
    for neg_ref in neg_refs:
        neg = neg_ref[...]
        scores = dot(query_bf, neg, NT) * inv_scale
        weight = (jax.nn.sigmoid(scores) * inv_scale).astype(BF16)
        query_grad = query_grad + dot(weight, neg)
    ctx_grad = (pos_weight * query).astype(BF16)
    mixed_cot = norm_pull(mixed, out_gain_ref[...], query_grad)
    hidden_cot = dot(mixed_cot.astype(BF16), down_ref[...], NT).astype(BF16).astype(F32)
    up_cot = (hidden_cot * silu_ref[...].astype(F32)).astype(BF16)
    gate_cot = (hidden_cot * slope_ref[...].astype(F32)).astype(BF16)
    normed_cot = dot(gate_cot, gate_ref[...], NT)
    normed_cot = normed_cot + dot(up_cot, up_ref[...], NT)
    normed_cot = normed_cot.astype(BF16).astype(F32)
    head_grad = mixed_cot + norm_pull(base_ref[...], in_gain_ref[...], normed_cot)
    head_grad = head_grad.astype(BF16)
    queries = query.shape[0]
    slot = slot_ref[...]
    block = stage_ref.shape[1]
    stores = []
    for part in range(stage_ref.shape[0]):
        start = part * block
        place = ones_where(iota((block, slot.shape[1]), 0) + start == slot)
        out = dot(place[:, :queries], head_grad) + dot(place[:, queries:], ctx_grad)
        stage_ref[part] = out.astype(BF16)
        store = pltpu.make_async_copy(
            stage_ref.at[part], out_ref.at[pl.ds(start, block)], out_sem.at[part]
        )
        store.start()
        stores.append(store)
    for store in stores:
        store.wait()


def neg_grad_kernel(inv_scale, pieces, blocks, *refs):
    query_refs, neg_refs = refs[:pieces], refs[pieces : pieces + blocks]
    before_refs, out_refs = refs[pieces + blocks : -blocks], refs[-blocks:]
    for i in reversed(range(blocks)):
        neg = neg_refs[i][...]
        total = before_refs[i][...] if before_refs else jnp.zeros(neg.shape, F32)
        for query_ref in query_refs:
            query = query_ref[...]
            scores = dot(neg, query, NT) * inv_scale
            weight = (jax.nn.sigmoid(scores) * inv_scale).astype(BF16)
            total = total + dot(weight, query)
        out_refs[i][...] = total.astype(out_refs[i].dtype)


def wanted_row_kernel(wanted_ref, out_ref):
    dev_count, capacity = wanted_ref.shape
    slots = out_ref.shape[1]
    high, low = split_bytes(wanted_ref[...].astype(F32))
    at = ones_where(
        lax.rem(iota((capacity, slots), 1), capacity) == iota((capacity, slots), 0)
    )
    spread = dot(high, at) * 256.0 + dot(low, at)
    first = iota((dev_count, slots), 0) * capacity
    slot = iota((dev_count, slots), 1)
    mine = (slot >= first) & (slot < first + capacity)
    out_ref[...] = jnp.sum(jnp.where(mine, spread, 0.0), axis=0, keepdims=True).astype(I32)


def scatter_kernel(wanted_ref, back_hbm, out_ref, back_ref, sem):
    halves = sem.shape[0]
    slots = back_ref.shape[0]
    half = slots // halves
    loads = load_all(
        [
            (back_hbm.at[pl.ds(i * half, half)], back_ref.at[pl.ds(i * half, half)])
            for i in range(halves)
        ],
        sem,
    )
    wanted = wanted_ref[...]
    rows = math.gcd(out_ref.shape[0], 256)
    for start in range(0, out_ref.shape[0], rows):
        place = ones_where(iota((rows, slots), 0) + start == wanted)
        if start == 0:
            out = jnp.zeros((rows, out_ref.shape[1]), F32)
            for i, load in enumerate(loads):
                load.wait()
                part = slice(i * half, (i + 1) * half)
                out = out + dot(place[:, part], back_ref[part, :])
        else:
            out = dot(place, back_ref[...])
        out_ref[start : start + rows, :] = out


def add_negatives_kernel(parts, *refs):
    sent_refs = refs[:parts]
    local_ref, own_ref, before_ref, out_ref, stage_ref, sem = refs[parts:]
    neg = own_ref[...]
    for sent_ref in sent_refs:
        neg = neg + sent_ref[...].astype(F32)
    neg = neg.astype(BF16)
    local = local_ref[...]
    blocks, rows, _ = stage_ref.shape
    stores = []
    for block in range(blocks):
        start = block * rows
        spot = ones_where(iota((rows, local.shape[1]), 0) + start == local)
        stage_ref[block] = before_ref[start : start + rows, :] + dot(spot, neg)
        store = pltpu.make_async_copy(
            stage_ref.at[block], out_ref.at[pl.ds(start, rows)], sem.at[block]
        )
        store.start()
        stores.append(store)
    for store in stores:
        store.wait()


def flip(block, axis, step):
    count = lax.axis_size(axis)
    return lax.ppermute(block, axis, [(i, i ^ step) for i in range(count)])


def spread_over(block, axis, others, before, between):
    held = {0: block}
    for other in sorted(others, key=lambda n: (bin(n).count("1"), -n)):
        step = other & -other
        source = held[other - step]
        hops = bin(other).count("1")
        if hops > 1:
            source, _ = lax.optimization_barrier((source, before if hops == 2 else between))
        held[other] = flip(source, axis, step)
    return held


def per_device(
    table,
    touch_owner,
    touch_local,
    query_rel,
    neg_local,
    rel_table,
    in_gain,
    out_gain,
    w_gate,
    w_up,
    w_down,
):
    axes = ("ent", "grp")
    dev_count = lax.axis_size("ent") * lax.axis_size("grp")
    refs = touch_local.shape[0]
    queries = refs // 2
    capacity = 2 * refs // dev_count
    slots = dev_count * capacity
    rows, width = table.shape
    hidden = w_gate.shape[1]
    negs = neg_local.shape[0]
    inv_scale = 1.0 / math.sqrt(width)
    shape = jax.ShapeDtypeStruct
    in_gain = in_gain.reshape(1, width)
    out_gain = out_gain.reshape(1, width)
    neg_row = neg_local.reshape(1, negs)

    group = lax.axis_size("grp")
    half = group // 2
    hbm = pl.BlockSpec(memory_space=pl.ANY)
    vmem = pl.BlockSpec(memory_space=pltpu.VMEM)

    parts = 8 if rows % 128 == 0 else 1
    requests, slot_row = call(
        route_kernel,
        (pltpu.VMEM((dev_count, capacity), I32), pltpu.VMEM((1, refs), I32)),
        in_hbm(touch_owner.reshape(1, refs), touch_local.reshape(1, refs)),
        2 * refs * refs * dev_count,
        8 * refs,
    )
    wanted = lax.all_to_all(requests, axes, split_axis=0, concat_axis=0, tiled=True)

    neg_rows, small_table = call(
        negatives_kernel,
        (pltpu.VMEM((negs, width), BF16), shape((rows, width), BF16)),
        in_hbm(neg_row, table),
        SHADOW_FLOPS,
        6 * rows * width,
        in_specs=[hbm, hbm],
        scratch_shapes=[
            pltpu.VMEM((1, negs), I32),
            pltpu.VMEM((parts, rows // parts, width), F32),
            pltpu.SemaphoreType.DMA,
            pltpu.SemaphoreType.DMA((parts,)),
        ],
    )
    rel_rows = call(
        relation_kernel,
        pltpu.HBM((queries, width), BF16),
        in_hbm(query_rel.reshape(1, queries), rel_table),
        SHADOW_FLOPS,
        2 * rel_table.size,
    )

    block = math.gcd(slots, 256)
    looked = call(
        fetch_kernel,
        pltpu.HBM((slots, width), BF16),
        (pltpu.with_memory_space_constraint(wanted, pltpu.VMEM), small_table),
        SHADOW_FLOPS,
        2 * (slots + rows) * width,
        out_specs=hbm,
        scratch_shapes=[
            pltpu.VMEM((slots // block, block, width), BF16),
            pltpu.SemaphoreType.DMA((slots // block,)),
        ],
    )
    neg_held = spread_over(neg_rows, "grp", range(1, group), looked, rel_rows)
    neg_pieces = [neg_held[other] for other in range(group)]
    fetched = lax.all_to_all(
        looked.reshape(dev_count, capacity, width), axes, split_axis=0, concat_axis=0, tiled=True
    ).reshape(slots, width)

    def buffer(array):
        return pltpu.VMEM(array.shape, array.dtype)

    sources = (slot_row, fetched, rel_rows, in_gain, out_gain, w_gate, w_up, w_down)
    kept = (slot_row, in_gain, out_gain, w_gate, w_up, w_down)
    outputs = (
        shape((queries, width), BF16),
        shape((queries, width), F32),
        shape((queries, width), BF16),
        shape((queries, width), F32),
        shape((queries, hidden), BF16),
        shape((queries, hidden), BF16),
    )
    early = neg_pieces[:-1]
    query_bf, base, ctx, mixed, silu, slope, *staged = call(
        functools.partial(encode_kernel, len(early)),
        outputs
        + (pltpu.VMEM((negs, width), BF16),) * len(early)
        + tuple(pltpu.VMEM(a.shape, a.dtype) for a in kept),
        (slot_row, fetched) + in_hbm(*sources[2:]) + tuple(early),
        2 * queries * width * (2 * slots + 3 * hidden),
        2 * (slots * width + 3 * width * hidden),
        in_specs=[hbm] * (8 + len(early)),
        out_specs=[vmem] * 6 + [hbm] * len(early) + [vmem] * len(kept),
        scratch_shapes=[buffer(a) for a in sources[1:3]]
        + [pltpu.SemaphoreType.DMA((7,)), pltpu.SemaphoreType.DMA((1 + len(early),))],
    )
    staged, kept = staged[: len(early)] + neg_pieces[-1:], staged[len(early) :]
    low = 1 if group > 2 else 0
    near = [query_bf, flip(query_bf, "grp", half)] + ([flip(query_bf, "grp", low)] if low else [])
    far = [flip(near[1], "grp", low)] if low else []
    others = [other for other in range(1, group) if not other & (low | half)]

    outgoing = call(
        functools.partial(grad_kernel, inv_scale, len(neg_pieces)),
        pltpu.HBM((slots, width), BF16),
        (query_bf, mixed, ctx, silu, slope, base, *staged, *kept),
        2 * queries * width * (2 * slots + 3 * hidden + 2 * negs * len(neg_pieces)),
        2 * (slots * width + 3 * width * hidden + negs * width * len(neg_pieces)),
        out_specs=hbm,
        scratch_shapes=[
            pltpu.VMEM((slots // block, block, width), BF16),
            pltpu.SemaphoreType.DMA((slots // block,)),
        ],
    )
    returned = lax.all_to_all(
        outgoing.reshape(dev_count, capacity, width), axes, split_axis=0, concat_axis=0, tiled=True
    ).reshape(slots, width)

    blocks = 1 + len(others)
    neg_blocks = [neg_held[other] for other in [0] + others]
    first = call(
        functools.partial(neg_grad_kernel, inv_scale, len(near), blocks),
        [shape((negs, width), F32)] * blocks,
        (*near, *neg_blocks),
        SHADOW_FLOPS,
        2 * (len(near) + blocks) * negs * width,
    )
    def add_far(i, out):
        return call(
            functools.partial(neg_grad_kernel, inv_scale, len(far), 1),
            (out,),
            (*far, neg_blocks[i], first[i]),
            4 * len(far) * queries * negs * width,
            2 * (len(far) + 1) * negs * width,
        )[0]

    sums = [add_far(i, shape((negs, width), BF16)) for i in range(1, blocks)]
    own = add_far(0, pltpu.VMEM((negs, width), F32))
    sent = [flip(block, "grp", other) for other, block in zip(others, sums)]
    wanted_row = call(
        wanted_row_kernel, pltpu.VMEM((1, slots), I32), (wanted,), slots * dev_count, 4 * slots
    )

    scattered = call(
        scatter_kernel,
        pltpu.VMEM((rows, width), F32),
        (wanted_row, returned),
        SHADOW_FLOPS,
        4 * rows * width + 2 * slots * width,
        in_specs=[vmem, hbm],
        scratch_shapes=[
            buffer(returned),
            pltpu.SemaphoreType.DMA((2 if slots % 32 == 0 else 1,)),
        ],
    )
    parts = 8 if rows % 128 == 0 else 1
    return call(
        functools.partial(add_negatives_kernel, len(sent)),
        shape((rows, width), F32),
        (*sent, neg_row, own, scattered),
        2 * rows * width * negs,
        8 * rows * width,
        out_specs=hbm,
        scratch_shapes=[
            pltpu.VMEM((parts, rows // parts, width), F32),
            pltpu.SemaphoreType.DMA((parts,)),
        ],
    )


def solution(mesh):
    return jax.shard_map(
        per_device,
        mesh=mesh,
        in_specs=(
            P(("ent", "grp"), None),
            P(("ent", "grp"), None),
            P(("ent", "grp")),
            P(("ent", "grp")),
            P(("ent", "grp")),
            P(),
            P(),
            P(),
            P(),
            P(),
            P(),
        ),
        out_specs=P(("ent", "grp"), None),
        check_vma=False,
    )
```

```python
import functools
import math

import jax
import jax.numpy as jnp
from jax import lax
from jax.experimental import pallas as pl
from jax.experimental.pallas import tpu as pltpu
from jax.sharding import PartitionSpec as P

POS_WEIGHT = 64

norm_eps = 1e-06

SHADOW_FLOPS = 1 << 45

F32 = jnp.float32
BF16 = jnp.bfloat16
I32 = jnp.int32

NN = (((1,), (0,)), ((), ()))
NT = (((1,), (1,)), ((), ()))
TN = (((0,), (0,)), ((), ()))


def dot(a, b, dims=NN):
    return lax.dot_general(a, b, dims, preferred_element_type=F32)


def in_hbm(*arrays):
    return tuple(pltpu.with_memory_space_constraint(array, pltpu.HBM) for array in arrays)


def iota(shape, axis):
    return lax.broadcasted_iota(I32, shape, axis)


def ones_where(mask):
    return jnp.where(mask, 1.0, 0.0).astype(BF16)


def to_column(row):
    count = row.shape[1]
    same = iota((count, count), 0) == iota((count, count), 1)
    return jnp.sum(jnp.where(same, row, 0.0), axis=1, keepdims=True)


def to_row(column):
    count = column.shape[0]
    same = iota((count, count), 0) == iota((count, count), 1)
    return jnp.sum(jnp.where(same, column, 0.0), axis=0, keepdims=True)


def split_bytes(numbers):
    high = jnp.floor(numbers * (1.0 / 256.0))
    return high.astype(BF16), (numbers - high * 256.0).astype(BF16)


def call(kernel, out_shape, args, flops, moved, **kwargs):
    return pl.pallas_call(
        kernel,
        out_shape=out_shape,
        compiler_params=pltpu.CompilerParams(vmem_limit_bytes=kwargs.pop("vmem", 28) << 20),
        cost_estimate=pl.CostEstimate(flops=flops, bytes_accessed=moved, transcendentals=0),
        **kwargs,
    )(*args)


def route_kernel(owner_ref, local_ref, request_ref, slot_ref):
    refs = owner_ref.shape[1]
    dev_count, capacity = request_ref.shape
    owner = owner_ref[...]
    hit = owner == iota((dev_count, refs), 0)
    earlier = ones_where(iota((refs, refs), 0) <= iota((refs, refs), 1))
    rank = dot(ones_where(hit), earlier)
    placed = jnp.sum(jnp.where(hit, rank, 0.0), axis=0, keepdims=True).astype(I32) - 1
    slot_ref[...] = owner * capacity + placed
    at = ones_where(iota((capacity, refs), 0) == placed)
    high, low = split_bytes(jnp.where(hit, local_ref[...].astype(F32), 0.0))
    request_ref[...] = (dot(high, at, NT) * 256.0 + dot(low, at, NT)).astype(I32)


def negatives_kernel(
    neg_local_hbm, table_ref, neg_ref, small_ref, neg_local_ref, stage_ref, local_sem, sem
):
    local_load = pltpu.make_async_copy(neg_local_hbm, neg_local_ref, local_sem)
    local_load.start()
    parts, rows, _ = stage_ref.shape
    copies = load_all(
        [
            (table_ref.at[pl.ds(part * rows, rows)], stage_ref.at[part])
            for part in range(parts)
        ],
        sem,
    )
    local_load.wait()
    neg_local = to_column(neg_local_ref[...].astype(F32)).astype(I32)
    total = jnp.zeros(neg_ref.shape, F32)
    for part, copy in enumerate(copies):
        copy.wait()
        small = stage_ref[part].astype(BF16)
        small_ref[part * rows : (part + 1) * rows, :] = small
        hot = neg_local == iota((neg_ref.shape[0], rows), 1) + part * rows
        total = total + dot(ones_where(hot), small)
    neg_ref[...] = total.astype(BF16)


def fetch_kernel(wanted_ref, table_ref, out_ref, stage_ref, sem):
    dev_count, capacity = wanted_ref.shape
    slots = out_ref.shape[0]
    rows = table_ref.shape[0]
    high, low = split_bytes(wanted_ref[...].astype(F32))
    first = iota((slots, dev_count), 1) * capacity
    slot = iota((slots, dev_count), 0)
    mine = ones_where((slot >= first) & (slot < first + capacity))
    spread = dot(mine, high) * 256.0 + dot(mine, low)
    at = lax.rem(iota((slots, capacity), 0), capacity) == iota((slots, capacity), 1)
    wanted = jnp.sum(jnp.where(at, spread, 0.0), axis=1, keepdims=True).astype(I32)
    block = stage_ref.shape[1]
    stores = []
    for part in range(stage_ref.shape[0]):
        start = part * block
        hot = ones_where(wanted[start : start + block] == iota((block, rows), 1))
        stage_ref[part] = dot(hot, table_ref[...]).astype(BF16)
        store = pltpu.make_async_copy(
            stage_ref.at[part], out_ref.at[pl.ds(start, block)], sem.at[part]
        )
        store.start()
        stores.append(store)
    for store in stores:
        store.wait()


def relation_kernel(rel_ref, table_ref, out_ref):
    rel = to_column(rel_ref[...].astype(F32)).astype(I32)
    hot = ones_where(rel == iota((rel.shape[0], table_ref.shape[0]), 1))
    out_ref[...] = dot(hot, table_ref[...]).astype(BF16)


def load_all(pairs, sem):
    copies = [
        pltpu.make_async_copy(source, buffer, sem.at[i])
        for i, (source, buffer) in enumerate(pairs)
    ]
    for copy in copies:
        copy.start()
    return copies


def encode_kernel(pieces, *refs):
    sources = refs[:8]
    neg_sources = refs[8 : pieces + 8]
    query_bf_ref, base_ref, ctx_ref, mixed_ref, silu_ref, slope_ref = refs[pieces + 8 : pieces + 14]
    neg_refs = refs[pieces + 14 : 2 * pieces + 14]
    slot_ref, in_gain_ref, out_gain_ref, gate_ref, up_ref, down_ref = refs[
        2 * pieces + 14 : 2 * pieces + 20
    ]
    fetched_ref, rel_ref, sem, late_sem = refs[2 * pieces + 20 :]
    buffers = (slot_ref, fetched_ref, rel_ref, in_gain_ref, out_gain_ref, gate_ref, up_ref)
    loads = load_all(zip(sources[:7], buffers), sem)
    queries = rel_ref.shape[0]
    refs = slot_ref.shape[1]
    slots = fetched_ref.shape[0]
    loads[0].wait()
    slot = to_column(slot_ref[...].astype(F32)).astype(I32)
    pick = ones_where(slot == iota((refs, slots), 1))
    loads[1].wait()
    head = dot(pick[:queries], fetched_ref[...])
    for load in loads[2:5]:
        load.wait()
    base = head + rel_ref[...].astype(F32)
    base_ref[...] = base
    in_scale = lax.rsqrt(jnp.mean(base * base, axis=-1, keepdims=True) + norm_eps)
    normed = (base * in_scale * in_gain_ref[...]).astype(BF16)
    ctx_ref[...] = dot(pick[queries:], fetched_ref[...]).astype(BF16)
    loads[5].wait()
    late = load_all(((sources[7], down_ref), *zip(neg_sources, neg_refs)), late_sem)
    gate = dot(normed, gate_ref[...])
    loads[6].wait()
    up = dot(normed, up_ref[...])
    sig = jax.nn.sigmoid(gate)
    silu = gate * sig
    hidden = (silu * up).astype(BF16)
    silu_ref[...] = silu.astype(BF16)
    slope_ref[...] = (up * (sig + silu * (1.0 - sig))).astype(BF16)
    late[0].wait()
    mixed = base + dot(hidden, down_ref[...])
    mixed_ref[...] = mixed
    out_scale = lax.rsqrt(jnp.mean(mixed * mixed, axis=-1, keepdims=True) + norm_eps)
    query_bf_ref[...] = (mixed * out_scale * out_gain_ref[...]).astype(BF16)
    for load in late[1:]:
        load.wait()


def norm_pull(value, gain, cotangent):
    scale = lax.rsqrt(jnp.mean(value * value, axis=-1, keepdims=True) + norm_eps)
    scaled = cotangent * gain
    along = jnp.mean(scaled * value, axis=-1, keepdims=True)
    return scale * scaled - value * (along * scale * scale * scale)


def grad_kernel(inv_scale, pieces, *refs):
    query_ref, mixed_ref, ctx_ref, silu_ref, slope_ref, base_ref = refs[:6]
    neg_refs = refs[6 : pieces + 6]
    slot_ref, in_gain_ref, out_gain_ref, gate_ref, up_ref, down_ref = refs[
        pieces + 6 : pieces + 12
    ]
    out_ref, stage_ref, out_sem = refs[pieces + 12 :]
    mixed = mixed_ref[...]
    out_scale = lax.rsqrt(jnp.mean(mixed * mixed, axis=-1, keepdims=True) + norm_eps)
    query = mixed * out_scale * out_gain_ref[...]
    query_bf = query_ref[...]
    ctx = ctx_ref[...].astype(F32)
    pos_score = jnp.sum(query * ctx, axis=-1, keepdims=True) * inv_scale
    pos_weight = POS_WEIGHT * (jax.nn.sigmoid(pos_score) - 1.0) * inv_scale
    query_grad = pos_weight * ctx
    for neg_ref in neg_refs:
        neg = neg_ref[...]
        scores = dot(query_bf, neg, NT) * inv_scale
        weight = (jax.nn.sigmoid(scores) * inv_scale).astype(BF16)
        query_grad = query_grad + dot(weight, neg)
    ctx_grad = (pos_weight * query).astype(BF16)
    mixed_cot = norm_pull(mixed, out_gain_ref[...], query_grad)
    hidden_cot = dot(mixed_cot.astype(BF16), down_ref[...], NT).astype(BF16).astype(F32)
    up_cot = (hidden_cot * silu_ref[...].astype(F32)).astype(BF16)
    gate_cot = (hidden_cot * slope_ref[...].astype(F32)).astype(BF16)
    normed_cot = dot(gate_cot, gate_ref[...], NT)
    normed_cot = normed_cot + dot(up_cot, up_ref[...], NT)
    normed_cot = normed_cot.astype(BF16).astype(F32)
    head_grad = mixed_cot + norm_pull(base_ref[...], in_gain_ref[...], normed_cot)
    head_grad = head_grad.astype(BF16)
    queries = query.shape[0]
    slot = slot_ref[...]
    block = stage_ref.shape[1]
    stores = []
    for part in range(stage_ref.shape[0]):
        start = part * block
        place = ones_where(iota((block, slot.shape[1]), 0) + start == slot)
        out = dot(place[:, :queries], head_grad) + dot(place[:, queries:], ctx_grad)
        stage_ref[part] = out.astype(BF16)
        store = pltpu.make_async_copy(
            stage_ref.at[part], out_ref.at[pl.ds(start, block)], out_sem.at[part]
        )
        store.start()
        stores.append(store)
    for store in stores:
        store.wait()


def neg_grad_kernel(inv_scale, pieces, blocks, *refs):
    query_refs, neg_refs = refs[:pieces], refs[pieces : pieces + blocks]
    before_refs, out_refs = refs[pieces + blocks : -blocks], refs[-blocks:]
    for i in reversed(range(blocks)):
        neg = neg_refs[i][...]
        total = before_refs[i][...] if before_refs else jnp.zeros(neg.shape, F32)
        for query_ref in query_refs:
            query = query_ref[...]
            scores = dot(neg, query, NT) * inv_scale
            weight = (jax.nn.sigmoid(scores) * inv_scale).astype(BF16)
            total = total + dot(weight, query)
        out_refs[i][...] = total.astype(out_refs[i].dtype)


def wanted_row_kernel(wanted_ref, out_ref):
    dev_count, capacity = wanted_ref.shape
    slots = out_ref.shape[1]
    high, low = split_bytes(wanted_ref[...].astype(F32))
    at = ones_where(
        lax.rem(iota((capacity, slots), 1), capacity) == iota((capacity, slots), 0)
    )
    spread = dot(high, at) * 256.0 + dot(low, at)
    first = iota((dev_count, slots), 0) * capacity
    slot = iota((dev_count, slots), 1)
    mine = (slot >= first) & (slot < first + capacity)
    out_ref[...] = jnp.sum(jnp.where(mine, spread, 0.0), axis=0, keepdims=True).astype(I32)


def scatter_kernel(wanted_ref, back_hbm, out_ref, back_ref, sem):
    halves = sem.shape[0]
    slots = back_ref.shape[0]
    half = slots // halves
    loads = load_all(
        [
            (back_hbm.at[pl.ds(i * half, half)], back_ref.at[pl.ds(i * half, half)])
            for i in range(halves)
        ],
        sem,
    )
    wanted = wanted_ref[...]
    rows = math.gcd(out_ref.shape[0], 256)
    for start in range(0, out_ref.shape[0], rows):
        place = ones_where(iota((rows, slots), 0) + start == wanted)
        if start == 0:
            out = jnp.zeros((rows, out_ref.shape[1]), F32)
            for i, load in enumerate(loads):
                load.wait()
                part = slice(i * half, (i + 1) * half)
                out = out + dot(place[:, part], back_ref[part, :])
        else:
            out = dot(place, back_ref[...])
        out_ref[start : start + rows, :] = out


def add_negatives_kernel(parts, *refs):
    sent_refs = refs[:parts]
    local_ref, own_ref, before_ref, out_ref, stage_ref, sem = refs[parts:]
    neg = own_ref[...]
    for sent_ref in sent_refs:
        neg = neg + sent_ref[...].astype(F32)
    neg = neg.astype(BF16)
    local = local_ref[...]
    blocks, rows, _ = stage_ref.shape
    stores = []
    for block in range(blocks):
        start = block * rows
        spot = ones_where(iota((rows, local.shape[1]), 0) + start == local)
        stage_ref[block] = before_ref[start : start + rows, :] + dot(spot, neg)
        store = pltpu.make_async_copy(
            stage_ref.at[block], out_ref.at[pl.ds(start, rows)], sem.at[block]
        )
        store.start()
        stores.append(store)
    for store in stores:
        store.wait()


def flip(block, axis, step):
    count = lax.axis_size(axis)
    return lax.ppermute(block, axis, [(i, i ^ step) for i in range(count)])


def spread_over(block, axis, others, before, between):
    held = {0: block}
    for other in sorted(others, key=lambda n: (bin(n).count("1"), -n)):
        hops = bin(other).count("1")
        rest = other & (other - 1) if hops > 2 else other
        step = rest & -rest
        source = held[other - step]
        if hops > 1:
            source, _ = lax.optimization_barrier((source, before if hops == 2 else between))
        held[other] = flip(source, axis, step)
    return held


def per_device(
    table,
    touch_owner,
    touch_local,
    query_rel,
    neg_local,
    rel_table,
    in_gain,
    out_gain,
    w_gate,
    w_up,
    w_down,
):
    axes = ("ent", "grp")
    dev_count = lax.axis_size("ent") * lax.axis_size("grp")
    refs = touch_local.shape[0]
    queries = refs // 2
    capacity = 2 * refs // dev_count
    slots = dev_count * capacity
    rows, width = table.shape
    hidden = w_gate.shape[1]
    negs = neg_local.shape[0]
    inv_scale = 1.0 / math.sqrt(width)
    shape = jax.ShapeDtypeStruct
    in_gain = in_gain.reshape(1, width)
    out_gain = out_gain.reshape(1, width)
    neg_row = neg_local.reshape(1, negs)

    group = lax.axis_size("grp")
    half = group // 2
    hbm = pl.BlockSpec(memory_space=pl.ANY)
    vmem = pl.BlockSpec(memory_space=pltpu.VMEM)

    parts = 8 if rows % 128 == 0 else 1
    requests, slot_row = call(
        route_kernel,
        (pltpu.VMEM((dev_count, capacity), I32), pltpu.VMEM((1, refs), I32)),
        in_hbm(touch_owner.reshape(1, refs), touch_local.reshape(1, refs)),
        2 * refs * refs * dev_count,
        8 * refs,
    )
    wanted = lax.all_to_all(requests, axes, split_axis=0, concat_axis=0, tiled=True)

    neg_rows, small_table = call(
        negatives_kernel,
        (pltpu.VMEM((negs, width), BF16), shape((rows, width), BF16)),
        in_hbm(neg_row, table),
        SHADOW_FLOPS,
        6 * rows * width,
        in_specs=[hbm, hbm],
        scratch_shapes=[
            pltpu.VMEM((1, negs), I32),
            pltpu.VMEM((parts, rows // parts, width), F32),
            pltpu.SemaphoreType.DMA,
            pltpu.SemaphoreType.DMA((parts,)),
        ],
    )
    rel_rows = call(
        relation_kernel,
        pltpu.HBM((queries, width), BF16),
        in_hbm(query_rel.reshape(1, queries), rel_table),
        SHADOW_FLOPS,
        2 * rel_table.size,
    )

    block = math.gcd(slots, 256)
    looked = call(
        fetch_kernel,
        pltpu.HBM((slots, width), BF16),
        (pltpu.with_memory_space_constraint(wanted, pltpu.VMEM), small_table),
        SHADOW_FLOPS,
        2 * (slots + rows) * width,
        out_specs=hbm,
        scratch_shapes=[
            pltpu.VMEM((slots // block, block, width), BF16),
            pltpu.SemaphoreType.DMA((slots // block,)),
        ],
    )
    neg_held = spread_over(neg_rows, "grp", range(1, group), looked, rel_rows)
    neg_pieces = [neg_held[other] for other in range(group)]
    fetched = lax.all_to_all(
        looked.reshape(dev_count, capacity, width), axes, split_axis=0, concat_axis=0, tiled=True
    ).reshape(slots, width)

    def buffer(array):
        return pltpu.VMEM(array.shape, array.dtype)

    sources = (slot_row, fetched, rel_rows, in_gain, out_gain, w_gate, w_up, w_down)
    kept = (slot_row, in_gain, out_gain, w_gate, w_up, w_down)
    outputs = (
        shape((queries, width), BF16),
        shape((queries, width), F32),
        shape((queries, width), BF16),
        shape((queries, width), F32),
        shape((queries, hidden), BF16),
        shape((queries, hidden), BF16),
    )
    early = neg_pieces[:-1]
    query_bf, base, ctx, mixed, silu, slope, *staged = call(
        functools.partial(encode_kernel, len(early)),
        outputs
        + (pltpu.VMEM((negs, width), BF16),) * len(early)
        + tuple(pltpu.VMEM(a.shape, a.dtype) for a in kept),
        (slot_row, fetched) + in_hbm(*sources[2:]) + tuple(early),
        2 * queries * width * (2 * slots + 3 * hidden),
        2 * (slots * width + 3 * width * hidden),
        in_specs=[hbm] * (8 + len(early)),
        out_specs=[vmem] * 6 + [hbm] * len(early) + [vmem] * len(kept),
        scratch_shapes=[buffer(a) for a in sources[1:3]]
        + [pltpu.SemaphoreType.DMA((7,)), pltpu.SemaphoreType.DMA((1 + len(early),))],
    )
    staged, kept = staged[: len(early)] + neg_pieces[-1:], staged[len(early) :]
    low = 1 if group > 2 else 0
    near = [query_bf, flip(query_bf, "grp", half)] + ([flip(query_bf, "grp", low)] if low else [])
    far = [flip(near[1], "grp", low)] if low else []
    others = [other for other in range(1, group) if not other & (low | half)]

    outgoing = call(
        functools.partial(grad_kernel, inv_scale, len(neg_pieces)),
        pltpu.HBM((slots, width), BF16),
        (query_bf, mixed, ctx, silu, slope, base, *staged, *kept),
        2 * queries * width * (2 * slots + 3 * hidden + 2 * negs * len(neg_pieces)),
        2 * (slots * width + 3 * width * hidden + negs * width * len(neg_pieces)),
        out_specs=hbm,
        scratch_shapes=[
            pltpu.VMEM((slots // block, block, width), BF16),
            pltpu.SemaphoreType.DMA((slots // block,)),
        ],
    )
    returned = lax.all_to_all(
        outgoing.reshape(dev_count, capacity, width), axes, split_axis=0, concat_axis=0, tiled=True
    ).reshape(slots, width)

    blocks = 1 + len(others)
    neg_blocks = [neg_held[other] for other in [0] + others]
    first = call(
        functools.partial(neg_grad_kernel, inv_scale, len(near), blocks),
        [shape((negs, width), F32)] * blocks,
        (*near, *neg_blocks),
        SHADOW_FLOPS,
        2 * (len(near) + blocks) * negs * width,
    )
    def add_far(i, out):
        return call(
            functools.partial(neg_grad_kernel, inv_scale, len(far), 1),
            (out,),
            (*far, neg_blocks[i], first[i]),
            4 * len(far) * queries * negs * width,
            2 * (len(far) + 1) * negs * width,
        )[0]

    sums = [add_far(i, shape((negs, width), BF16)) for i in range(1, blocks)]
    own = add_far(0, pltpu.VMEM((negs, width), F32))
    sent = [flip(block, "grp", other) for other, block in zip(others, sums)]
    wanted, _ = lax.optimization_barrier((wanted, near[1]))
    wanted_row = call(
        wanted_row_kernel, pltpu.VMEM((1, slots), I32), (wanted,), slots * dev_count, 4 * slots
    )

    scattered = call(
        scatter_kernel,
        pltpu.VMEM((rows, width), F32),
        (wanted_row, returned),
        SHADOW_FLOPS,
        4 * rows * width + 2 * slots * width,
        in_specs=[vmem, hbm],
        scratch_shapes=[
            buffer(returned),
            pltpu.SemaphoreType.DMA((2 if slots % 32 == 0 else 1,)),
        ],
    )
    parts = 8 if rows % 128 == 0 else 1
    return call(
        functools.partial(add_negatives_kernel, len(sent)),
        shape((rows, width), F32),
        (*sent, neg_row, own, scattered),
        2 * rows * width * negs,
        8 * rows * width,
        out_specs=hbm,
        scratch_shapes=[
            pltpu.VMEM((parts, rows // parts, width), F32),
            pltpu.SemaphoreType.DMA((parts,)),
        ],
    )


def solution(mesh):
    return jax.shard_map(
        per_device,
        mesh=mesh,
        in_specs=(
            P(("ent", "grp"), None),
            P(("ent", "grp"), None),
            P(("ent", "grp")),
            P(("ent", "grp")),
            P(("ent", "grp")),
            P(),
            P(),
            P(),
            P(),
            P(),
            P(),
        ),
        out_specs=P(("ent", "grp"), None),
        check_vma=False,
    )
```

```python
import functools
import math

import jax
import jax.numpy as jnp
from jax import lax
from jax.experimental import pallas as pl
from jax.experimental.pallas import tpu as pltpu
from jax.sharding import PartitionSpec as P

POS_WEIGHT = 64

norm_eps = 1e-06

SHADOW_FLOPS = 1 << 45

F32 = jnp.float32
BF16 = jnp.bfloat16
I32 = jnp.int32

NN = (((1,), (0,)), ((), ()))
NT = (((1,), (1,)), ((), ()))
TN = (((0,), (0,)), ((), ()))


def dot(a, b, dims=NN):
    return lax.dot_general(a, b, dims, preferred_element_type=F32)


def in_hbm(*arrays):
    return tuple(pltpu.with_memory_space_constraint(array, pltpu.HBM) for array in arrays)


def iota(shape, axis):
    return lax.broadcasted_iota(I32, shape, axis)


def ones_where(mask):
    return jnp.where(mask, 1.0, 0.0).astype(BF16)


def to_column(row):
    count = row.shape[1]
    same = iota((count, count), 0) == iota((count, count), 1)
    return jnp.sum(jnp.where(same, row, 0.0), axis=1, keepdims=True)


def to_row(column):
    count = column.shape[0]
    same = iota((count, count), 0) == iota((count, count), 1)
    return jnp.sum(jnp.where(same, column, 0.0), axis=0, keepdims=True)


def split_bytes(numbers):
    high = jnp.floor(numbers * (1.0 / 256.0))
    return high.astype(BF16), (numbers - high * 256.0).astype(BF16)


def call(kernel, out_shape, args, flops, moved, **kwargs):
    return pl.pallas_call(
        kernel,
        out_shape=out_shape,
        compiler_params=pltpu.CompilerParams(vmem_limit_bytes=kwargs.pop("vmem", 28) << 20),
        cost_estimate=pl.CostEstimate(flops=flops, bytes_accessed=moved, transcendentals=0),
        **kwargs,
    )(*args)


def route_kernel(owner_ref, local_ref, request_ref, slot_ref):
    refs = owner_ref.shape[1]
    dev_count, capacity = request_ref.shape
    owner = owner_ref[...]
    hit = owner == iota((dev_count, refs), 0)
    earlier = ones_where(iota((refs, refs), 0) <= iota((refs, refs), 1))
    rank = dot(ones_where(hit), earlier)
    placed = jnp.sum(jnp.where(hit, rank, 0.0), axis=0, keepdims=True).astype(I32) - 1
    slot_ref[...] = owner * capacity + placed
    at = ones_where(iota((capacity, refs), 0) == placed)
    high, low = split_bytes(jnp.where(hit, local_ref[...].astype(F32), 0.0))
    request_ref[...] = (dot(high, at, NT) * 256.0 + dot(low, at, NT)).astype(I32)


def negatives_kernel(
    neg_local_hbm, table_ref, neg_ref, small_ref, neg_local_ref, stage_ref, local_sem, sem
):
    local_load = pltpu.make_async_copy(neg_local_hbm, neg_local_ref, local_sem)
    local_load.start()
    parts, rows, _ = stage_ref.shape
    copies = load_all(
        [
            (table_ref.at[pl.ds(part * rows, rows)], stage_ref.at[part])
            for part in range(parts)
        ],
        sem,
    )
    local_load.wait()
    neg_local = to_column(neg_local_ref[...].astype(F32)).astype(I32)
    total = jnp.zeros(neg_ref.shape, F32)
    for part, copy in enumerate(copies):
        copy.wait()
        small = stage_ref[part].astype(BF16)
        small_ref[part * rows : (part + 1) * rows, :] = small
        hot = neg_local == iota((neg_ref.shape[0], rows), 1) + part * rows
        total = total + dot(ones_where(hot), small)
    neg_ref[...] = total.astype(BF16)


def fetch_kernel(wanted_ref, table_ref, out_ref, stage_ref, sem):
    dev_count, capacity = wanted_ref.shape
    slots = out_ref.shape[0]
    rows = table_ref.shape[0]
    high, low = split_bytes(wanted_ref[...].astype(F32))
    first = iota((slots, dev_count), 1) * capacity
    slot = iota((slots, dev_count), 0)
    mine = ones_where((slot >= first) & (slot < first + capacity))
    spread = dot(mine, high) * 256.0 + dot(mine, low)
    at = lax.rem(iota((slots, capacity), 0), capacity) == iota((slots, capacity), 1)
    wanted = jnp.sum(jnp.where(at, spread, 0.0), axis=1, keepdims=True).astype(I32)
    block = stage_ref.shape[1]
    stores = []
    for part in range(stage_ref.shape[0]):
        start = part * block
        hot = ones_where(wanted[start : start + block] == iota((block, rows), 1))
        stage_ref[part] = dot(hot, table_ref[...]).astype(BF16)
        store = pltpu.make_async_copy(
            stage_ref.at[part], out_ref.at[pl.ds(start, block)], sem.at[part]
        )
        store.start()
        stores.append(store)
    for store in stores:
        store.wait()


def relation_kernel(rel_ref, table_ref, out_ref):
    rel = to_column(rel_ref[...].astype(F32)).astype(I32)
    hot = ones_where(rel == iota((rel.shape[0], table_ref.shape[0]), 1))
    out_ref[...] = dot(hot, table_ref[...]).astype(BF16)


def load_all(pairs, sem):
    copies = [
        pltpu.make_async_copy(source, buffer, sem.at[i])
        for i, (source, buffer) in enumerate(pairs)
    ]
    for copy in copies:
        copy.start()
    return copies


def encode_kernel(pieces, *refs):
    sources = refs[:8]
    neg_sources = refs[8 : pieces + 8]
    query_bf_ref, base_ref, ctx_ref, mixed_ref, silu_ref, slope_ref = refs[pieces + 8 : pieces + 14]
    neg_refs = refs[pieces + 14 : 2 * pieces + 14]
    slot_ref, in_gain_ref, out_gain_ref, gate_ref, up_ref, down_ref = refs[
        2 * pieces + 14 : 2 * pieces + 20
    ]
    fetched_ref, rel_ref, sem, late_sem = refs[2 * pieces + 20 :]
    buffers = (slot_ref, fetched_ref, rel_ref, in_gain_ref, out_gain_ref, gate_ref, up_ref)
    loads = load_all(zip(sources[:7], buffers), sem)
    queries = rel_ref.shape[0]
    refs = slot_ref.shape[1]
    slots = fetched_ref.shape[0]
    loads[0].wait()
    slot = to_column(slot_ref[...].astype(F32)).astype(I32)
    pick = ones_where(slot == iota((refs, slots), 1))
    loads[1].wait()
    head = dot(pick[:queries], fetched_ref[...])
    for load in loads[2:5]:
        load.wait()
    base = head + rel_ref[...].astype(F32)
    base_ref[...] = base
    in_scale = lax.rsqrt(jnp.mean(base * base, axis=-1, keepdims=True) + norm_eps)
    normed = (base * in_scale * in_gain_ref[...]).astype(BF16)
    ctx_ref[...] = dot(pick[queries:], fetched_ref[...]).astype(BF16)
    loads[5].wait()
    late = load_all(((sources[7], down_ref), *zip(neg_sources, neg_refs)), late_sem)
    gate = dot(normed, gate_ref[...])
    loads[6].wait()
    up = dot(normed, up_ref[...])
    sig = jax.nn.sigmoid(gate)
    silu = gate * sig
    hidden = (silu * up).astype(BF16)
    silu_ref[...] = silu.astype(BF16)
    slope_ref[...] = (up * (sig + silu * (1.0 - sig))).astype(BF16)
    late[0].wait()
    mixed = base + dot(hidden, down_ref[...])
    mixed_ref[...] = mixed
    out_scale = lax.rsqrt(jnp.mean(mixed * mixed, axis=-1, keepdims=True) + norm_eps)
    query_bf_ref[...] = (mixed * out_scale * out_gain_ref[...]).astype(BF16)
    for load in late[1:]:
        load.wait()


def norm_pull(value, gain, cotangent):
    scale = lax.rsqrt(jnp.mean(value * value, axis=-1, keepdims=True) + norm_eps)
    scaled = cotangent * gain
    along = jnp.mean(scaled * value, axis=-1, keepdims=True)
    return scale * scaled - value * (along * scale * scale * scale)


def grad_kernel(inv_scale, pieces, *refs):
    query_ref, mixed_ref, ctx_ref, silu_ref, slope_ref, base_ref = refs[:6]
    neg_refs = refs[6 : pieces + 6]
    slot_ref, in_gain_ref, out_gain_ref, gate_ref, up_ref, down_ref = refs[
        pieces + 6 : pieces + 12
    ]
    out_ref, stage_ref, out_sem = refs[pieces + 12 :]
    mixed = mixed_ref[...]
    out_scale = lax.rsqrt(jnp.mean(mixed * mixed, axis=-1, keepdims=True) + norm_eps)
    query = mixed * out_scale * out_gain_ref[...]
    query_bf = query_ref[...]
    ctx = ctx_ref[...].astype(F32)
    pos_score = jnp.sum(query * ctx, axis=-1, keepdims=True) * inv_scale
    pos_weight = POS_WEIGHT * (jax.nn.sigmoid(pos_score) - 1.0) * inv_scale
    query_grad = pos_weight * ctx
    for neg_ref in neg_refs:
        neg = neg_ref[...]
        scores = dot(query_bf, neg, NT) * inv_scale
        weight = (jax.nn.sigmoid(scores) * inv_scale).astype(BF16)
        query_grad = query_grad + dot(weight, neg)
    ctx_grad = (pos_weight * query).astype(BF16)
    mixed_cot = norm_pull(mixed, out_gain_ref[...], query_grad)
    hidden_cot = dot(mixed_cot.astype(BF16), down_ref[...], NT).astype(BF16).astype(F32)
    up_cot = (hidden_cot * silu_ref[...].astype(F32)).astype(BF16)
    gate_cot = (hidden_cot * slope_ref[...].astype(F32)).astype(BF16)
    normed_cot = dot(gate_cot, gate_ref[...], NT)
    normed_cot = normed_cot + dot(up_cot, up_ref[...], NT)
    normed_cot = normed_cot.astype(BF16).astype(F32)
    head_grad = mixed_cot + norm_pull(base_ref[...], in_gain_ref[...], normed_cot)
    head_grad = head_grad.astype(BF16)
    queries = query.shape[0]
    slot = slot_ref[...]
    block = stage_ref.shape[1]
    stores = []
    for part in range(stage_ref.shape[0]):
        start = part * block
        place = ones_where(iota((block, slot.shape[1]), 0) + start == slot)
        out = dot(place[:, :queries], head_grad) + dot(place[:, queries:], ctx_grad)
        stage_ref[part] = out.astype(BF16)
        store = pltpu.make_async_copy(
            stage_ref.at[part], out_ref.at[pl.ds(start, block)], out_sem.at[part]
        )
        store.start()
        stores.append(store)
    for store in stores:
        store.wait()


def neg_grad_kernel(inv_scale, pieces, blocks, *refs):
    query_refs, neg_refs = refs[:pieces], refs[pieces : pieces + blocks]
    before_refs, out_refs = refs[pieces + blocks : -blocks], refs[-blocks:]
    for i in reversed(range(blocks)):
        neg = neg_refs[i][...]
        total = before_refs[i][...] if before_refs else jnp.zeros(neg.shape, F32)
        for query_ref in query_refs:
            query = query_ref[...]
            scores = dot(neg, query, NT) * inv_scale
            weight = (jax.nn.sigmoid(scores) * inv_scale).astype(BF16)
            total = total + dot(weight, query)
        out_refs[i][...] = total.astype(out_refs[i].dtype)


def wanted_row_kernel(wanted_ref, out_ref):
    dev_count, capacity = wanted_ref.shape
    slots = out_ref.shape[1]
    high, low = split_bytes(wanted_ref[...].astype(F32))
    at = ones_where(
        lax.rem(iota((capacity, slots), 1), capacity) == iota((capacity, slots), 0)
    )
    spread = dot(high, at) * 256.0 + dot(low, at)
    first = iota((dev_count, slots), 0) * capacity
    slot = iota((dev_count, slots), 1)
    mine = (slot >= first) & (slot < first + capacity)
    out_ref[...] = jnp.sum(jnp.where(mine, spread, 0.0), axis=0, keepdims=True).astype(I32)


def scatter_kernel(wanted_ref, back_hbm, out_ref, back_ref, sem):
    halves = sem.shape[0]
    slots = back_ref.shape[0]
    half = slots // halves
    loads = load_all(
        [
            (back_hbm.at[pl.ds(i * half, half)], back_ref.at[pl.ds(i * half, half)])
            for i in range(halves)
        ],
        sem,
    )
    wanted = wanted_ref[...]
    rows = math.gcd(out_ref.shape[0], 256)
    for start in range(0, out_ref.shape[0], rows):
        place = ones_where(iota((rows, slots), 0) + start == wanted)
        if start == 0:
            out = jnp.zeros((rows, out_ref.shape[1]), F32)
            for i, load in enumerate(loads):
                load.wait()
                part = slice(i * half, (i + 1) * half)
                out = out + dot(place[:, part], back_ref[part, :])
        else:
            out = dot(place, back_ref[...])
        out_ref[start : start + rows, :] = out


def add_negatives_kernel(parts, *refs):
    sent_refs = refs[:parts]
    local_ref, own_ref, before_ref, out_ref, stage_ref, sem = refs[parts:]
    neg = own_ref[...]
    for sent_ref in sent_refs:
        neg = neg + sent_ref[...].astype(F32)
    neg = neg.astype(BF16)
    local = local_ref[...]
    blocks, rows, _ = stage_ref.shape
    stores = []
    for block in range(blocks):
        start = block * rows
        spot = ones_where(iota((rows, local.shape[1]), 0) + start == local)
        stage_ref[block] = before_ref[start : start + rows, :] + dot(spot, neg)
        store = pltpu.make_async_copy(
            stage_ref.at[block], out_ref.at[pl.ds(start, rows)], sem.at[block]
        )
        store.start()
        stores.append(store)
    for store in stores:
        store.wait()


def flip(block, axis, step):
    count = lax.axis_size(axis)
    return lax.ppermute(block, axis, [(i, i ^ step) for i in range(count)])


def spread_over(block, axis, others, before, between):
    held = {0: block}
    for other in sorted(others, key=lambda n: (bin(n).count("1"), -n)):
        hops = bin(other).count("1")
        rest = other & (other - 1) if hops > 2 else other
        step = rest & -rest
        source = held[other - step]
        if hops > 1:
            source, _ = lax.optimization_barrier((source, before if hops == 2 else between))
        held[other] = flip(source, axis, step)
    return held


def per_device(
    table,
    touch_owner,
    touch_local,
    query_rel,
    neg_local,
    rel_table,
    in_gain,
    out_gain,
    w_gate,
    w_up,
    w_down,
):
    axes = ("ent", "grp")
    dev_count = lax.axis_size("ent") * lax.axis_size("grp")
    refs = touch_local.shape[0]
    queries = refs // 2
    capacity = 2 * refs // dev_count
    slots = dev_count * capacity
    rows, width = table.shape
    hidden = w_gate.shape[1]
    negs = neg_local.shape[0]
    inv_scale = 1.0 / math.sqrt(width)
    shape = jax.ShapeDtypeStruct
    in_gain = in_gain.reshape(1, width)
    out_gain = out_gain.reshape(1, width)
    neg_row = neg_local.reshape(1, negs)

    group = lax.axis_size("grp")
    half = group // 2
    hbm = pl.BlockSpec(memory_space=pl.ANY)
    vmem = pl.BlockSpec(memory_space=pltpu.VMEM)

    parts = 8 if rows % 128 == 0 else 1
    requests, slot_row = call(
        route_kernel,
        (pltpu.VMEM((dev_count, capacity), I32), pltpu.VMEM((1, refs), I32)),
        in_hbm(touch_owner.reshape(1, refs), touch_local.reshape(1, refs)),
        2 * refs * refs * dev_count,
        8 * refs,
    )
    wanted = lax.all_to_all(requests, axes, split_axis=0, concat_axis=0, tiled=True)

    neg_rows, small_table = call(
        negatives_kernel,
        (pltpu.VMEM((negs, width), BF16), shape((rows, width), BF16)),
        in_hbm(neg_row, table),
        SHADOW_FLOPS,
        6 * rows * width,
        in_specs=[hbm, hbm],
        scratch_shapes=[
            pltpu.VMEM((1, negs), I32),
            pltpu.VMEM((parts, rows // parts, width), F32),
            pltpu.SemaphoreType.DMA,
            pltpu.SemaphoreType.DMA((parts,)),
        ],
    )
    rel_rows = call(
        relation_kernel,
        pltpu.HBM((queries, width), BF16),
        in_hbm(query_rel.reshape(1, queries), rel_table),
        SHADOW_FLOPS,
        2 * rel_table.size,
    )

    block = math.gcd(slots, 256)
    looked = call(
        fetch_kernel,
        pltpu.HBM((slots, width), BF16),
        (pltpu.with_memory_space_constraint(wanted, pltpu.VMEM), small_table),
        SHADOW_FLOPS,
        2 * (slots + rows) * width,
        out_specs=hbm,
        scratch_shapes=[
            pltpu.VMEM((slots // block, block, width), BF16),
            pltpu.SemaphoreType.DMA((slots // block,)),
        ],
    )
    neg_held = spread_over(neg_rows, "grp", range(1, group), looked, rel_rows)
    neg_pieces = [neg_held[other] for other in range(group)]
    fetched = lax.all_to_all(
        looked.reshape(dev_count, capacity, width), axes, split_axis=0, concat_axis=0, tiled=True
    ).reshape(slots, width)

    def buffer(array):
        return pltpu.VMEM(array.shape, array.dtype)

    sources = (slot_row, fetched, rel_rows, in_gain, out_gain, w_gate, w_up, w_down)
    kept = (slot_row, in_gain, out_gain, w_gate, w_up, w_down)
    outputs = (
        shape((queries, width), BF16),
        shape((queries, width), F32),
        shape((queries, width), BF16),
        shape((queries, width), F32),
        shape((queries, hidden), BF16),
        shape((queries, hidden), BF16),
    )
    early = neg_pieces[:-1]
    query_bf, base, ctx, mixed, silu, slope, *staged = call(
        functools.partial(encode_kernel, len(early)),
        outputs
        + (pltpu.VMEM((negs, width), BF16),) * len(early)
        + tuple(pltpu.VMEM(a.shape, a.dtype) for a in kept),
        (slot_row, fetched) + in_hbm(*sources[2:]) + tuple(early),
        2 * queries * width * (2 * slots + 3 * hidden),
        2 * (slots * width + 3 * width * hidden),
        in_specs=[hbm] * (8 + len(early)),
        out_specs=[vmem] * 6 + [hbm] * len(early) + [vmem] * len(kept),
        scratch_shapes=[buffer(a) for a in sources[1:3]]
        + [pltpu.SemaphoreType.DMA((7,)), pltpu.SemaphoreType.DMA((1 + len(early),))],
    )
    staged, kept = staged[: len(early)] + neg_pieces[-1:], staged[len(early) :]
    low = 1 if group > 2 else 0
    near = [query_bf, flip(query_bf, "grp", half)] + ([flip(query_bf, "grp", low)] if low else [])
    far = [flip(near[1], "grp", low)] if low else []
    others = [other for other in range(1, group) if not other & (low | half)]

    outgoing = call(
        functools.partial(grad_kernel, inv_scale, len(neg_pieces)),
        pltpu.HBM((slots, width), BF16),
        (query_bf, mixed, ctx, silu, slope, base, *staged, *kept),
        2 * queries * width * (2 * slots + 3 * hidden + 2 * negs * len(neg_pieces)),
        2 * (slots * width + 3 * width * hidden + negs * width * len(neg_pieces)),
        out_specs=hbm,
        scratch_shapes=[
            pltpu.VMEM((slots // block, block, width), BF16),
            pltpu.SemaphoreType.DMA((slots // block,)),
        ],
    )
    returned = lax.all_to_all(
        outgoing.reshape(dev_count, capacity, width), axes, split_axis=0, concat_axis=0, tiled=True
    ).reshape(slots, width)

    blocks = 1 + len(others)
    neg_blocks = [neg_held[other] for other in [0] + others]
    first = call(
        functools.partial(neg_grad_kernel, inv_scale, len(near), blocks),
        [shape((negs, width), F32)] * blocks,
        (*near, *neg_blocks),
        SHADOW_FLOPS,
        2 * (len(near) + blocks) * negs * width,
    )
    def add_far(i, out):
        return call(
            functools.partial(neg_grad_kernel, inv_scale, len(far), 1),
            (out,),
            (*far, neg_blocks[i], first[i]),
            4 * len(far) * queries * negs * width,
            2 * (len(far) + 1) * negs * width,
        )[0]

    sums = [add_far(i, shape((negs, width), BF16)) for i in range(1, blocks)]
    own = add_far(0, pltpu.VMEM((negs, width), F32))
    sent = [flip(block, "grp", other) for other, block in zip(others, sums)]
    wanted, _ = lax.optimization_barrier((wanted, near[1]))
    wanted_row = call(
        wanted_row_kernel, pltpu.VMEM((1, slots), I32), (wanted,), slots * dev_count, 4 * slots
    )

    scattered = call(
        scatter_kernel,
        pltpu.VMEM((rows, width), F32),
        (wanted_row, returned),
        2 * rows * width * slots,
        4 * rows * width + 2 * slots * width,
        in_specs=[vmem, hbm],
        scratch_shapes=[
            buffer(returned),
            pltpu.SemaphoreType.DMA((2 if slots % 32 == 0 else 1,)),
        ],
    )
    parts = 8 if rows % 128 == 0 else 1
    return call(
        functools.partial(add_negatives_kernel, len(sent)),
        shape((rows, width), F32),
        (*sent, neg_row, own, scattered),
        2 * rows * width * negs,
        8 * rows * width,
        out_specs=hbm,
        scratch_shapes=[
            pltpu.VMEM((parts, rows // parts, width), F32),
            pltpu.SemaphoreType.DMA((parts,)),
        ],
    )


def solution(mesh):
    return jax.shard_map(
        per_device,
        mesh=mesh,
        in_specs=(
            P(("ent", "grp"), None),
            P(("ent", "grp"), None),
            P(("ent", "grp")),
            P(("ent", "grp")),
            P(("ent", "grp")),
            P(),
            P(),
            P(),
            P(),
            P(),
            P(),
        ),
        out_specs=P(("ent", "grp"), None),
        check_vma=False,
    )
```
